256 devices in a mesh: section: 8 (over z), dp: 32 (over y, x, core).
Axes of the slice: x: 4, y: 4, z: 8, core: 2. Of those that a mesh axis runs over, the one named last changes fastest.
Arguments:
- tokens: bfloat16 [32, 128, 4096], P('dp'), may hold values from -20 to 20
- kv_weight: bfloat16 [8, 4096, 1024], P('section'), may hold values from -0.09375 to 0.09375
- cache_kv: bfloat16 [8, 32, 128, 1024], P('section', 'dp'), may hold values from -5 to 5
- cached_len: int32 [32], P('dp'), may hold values from 8 to 128, as said below
- cotangent: bfloat16 [32, 128, 4096], P('dp'), may hold values from -6 to 6
Outputs:
- hidden_out: bfloat16 [8, 32, 128, 4096], P('section', 'dp')
- grad_stream: bfloat16 [8, 32, 128, 4096], P('section', 'dp')
- grad_kv: float32 [8, 4096, 1024], P('section', 'dp')
The draws below stay inside these ranges and needn't reach their ends.
Inputs may be any that keep to these rules, and one draw needn't show every extreme that they name: `cached_len`: some document has all 128 cached positions valid.
All inputs are finite; a program needn't handle non-finite values.
Results may differ from the reference program's by a relative error of at most 0.035.
Values may be sent and summed in bfloat16 or wider, within the bound.
No kernel may reach another device: no remote copies, remote signals or barrier semaphores. Data moves between devices by JAX's collectives and lax.ppermute only.
A program may use at most 128 MiB of HBM per device.

```python
import jax
import jax.numpy as jnp
from jax import lax

D = 4096
HEADS = 32
KV_HEADS = 4
HD = 128
PAST = 128
TOK = 128
KVW = 512
LAYERS = 8
DOCS = 32


def draw_tokens(key, part):
    key = jax.random.fold_in(key, 1)
    return jnp.clip(jax.random.normal(key, (DOCS, TOK, D), jnp.float32), -6.0, 6.0).astype(jnp.bfloat16)


def draw_cache_kv(key, part):
    key = jax.random.fold_in(key, 2)
    return jnp.clip(jax.random.normal(key, (LAYERS, DOCS, PAST, 2 * KVW), jnp.float32), -5.0, 5.0).astype(jnp.bfloat16)


def draw_cached_len(key, part):
    key = jax.random.fold_in(key, 3)
    lengths = jax.random.randint(jax.random.fold_in(key, 1), (DOCS,), 8, PAST + 1)
    chosen = jax.random.randint(jax.random.fold_in(key, 2), (), 0, DOCS)
    return lengths.at[chosen].set(PAST).astype(jnp.int32)


def levels(key, extent, pieces, low, largest):
    def one(position, parts):
        draws = jax.random.uniform(jax.random.fold_in(jax.random.fold_in(key, 6), position), (parts,), jnp.float32, low / len(pieces), largest / len(pieces))
        return jnp.repeat(jnp.exp(draws), extent[position] // parts).reshape((-1,) + (1,) * (len(extent) - position - 1))

    factor_of = one(*pieces[0])
    for cut in pieces[1:]:
        factor_of = factor_of * one(*cut)
    return factor_of


def bell_draw(key, extent, scale, bound, shards=(), kind=jnp.bfloat16):
    array = scale * jax.random.normal(key, extent, jnp.float32)
    if shards:
        array = array * levels(key, extent, shards, -0.22, 0.18)
    return jnp.clip(array, -bound, bound).astype(kind)


def setup_inputs(seed: int = 0) -> dict:
    arg_keys = jax.random.split(jax.random.key(seed), 6)
    return {
        "tokens": draw_tokens(jax.random.fold_in(arg_keys[5], 71), 0),
        "kv_weight": bell_draw(arg_keys[1], (LAYERS, D, 2 * KVW), D ** -0.5, 0.09375, ((0, 8),)),
        "cache_kv": draw_cache_kv(jax.random.fold_in(arg_keys[5], 71), 0),
        "cached_len": draw_cached_len(jax.random.fold_in(arg_keys[5], 71), 0),
        "cotangent": bell_draw(arg_keys[4], (DOCS, TOK, D), 1.0, 6.0, ((0, 32),)),
    }


norm_eps = 1e-06

def normalized(stream_in):
    stream_f = stream_in.astype(jnp.float32)
    inverse_rms = lax.rsqrt(lax.optimization_barrier(jnp.mean(stream_f * stream_f, axis=-1, keepdims=True)) + norm_eps)
    return (stream_f, inverse_rms)

def allowed_keys(first_row, row_count, length, past_rows, total_rows):
    query_pos = first_row + jnp.arange(row_count, dtype=jnp.int32)[:, None]
    key_pos = jnp.arange(past_rows + total_rows, dtype=jnp.int32)[None, :]
    cached_ok = key_pos < length
    window_ok = jnp.logical_and(key_pos >= past_rows, key_pos - past_rows <= query_pos)
    return jnp.where(key_pos < past_rows, cached_ok, window_ok)

def head_split(keys_all):
    key_count = keys_all.shape[0]
    half_width = keys_all.shape[1] // 2
    key_heads = keys_all[:, :half_width].reshape(key_count, KV_HEADS, HD)
    value_heads = keys_all[:, half_width:].reshape(key_count, KV_HEADS, HD)
    return (key_heads, value_heads)

def attention_weights(query_heads, key_heads, allowed):
    scores = jnp.einsum('qhgd,khd->hgqk', query_heads.astype(jnp.float32), key_heads.astype(jnp.float32)) * HD ** (-0.5)
    scores = jnp.where(allowed, scores, -1e+30)
    row_max = lax.optimization_barrier(jnp.max(scores, axis=-1, keepdims=True))
    expanded = jnp.exp(scores - row_max)
    return expanded / lax.optimization_barrier(jnp.sum(expanded, axis=-1, keepdims=True))

def layer_parts(stream_in, weight, cached, length):
    row_count = stream_in.shape[0]
    stream_f, inverse_rms = normalized(stream_in)
    normed = (stream_f * inverse_rms).astype(jnp.bfloat16)
    kv_new = jnp.dot(normed, weight, preferred_element_type=jnp.float32).astype(jnp.bfloat16)
    key_heads, value_heads = head_split(jnp.concatenate([cached, kv_new], axis=0))
    query_heads = normed.reshape(row_count, KV_HEADS, HEADS // KV_HEADS, HD)
    allowed = allowed_keys(0, row_count, length, PAST, row_count)
    probs = attention_weights(query_heads, key_heads, allowed)
    return (stream_f, inverse_rms, normed, key_heads, value_heads, query_heads, probs)

def layer_forward(stream_in, weight, cached, length):
    row_count = stream_in.shape[0]
    stream_f, inverse_rms, normed, key_heads, value_heads, query_heads, probs = layer_parts(stream_in, weight, cached, length)
    probs_low = probs.astype(jnp.bfloat16)
    mixed_out = jnp.einsum('hgqk,khd->qhgd', probs_low.astype(jnp.float32), value_heads.astype(jnp.float32)).reshape(row_count, D)
    return (stream_f + mixed_out).astype(jnp.bfloat16)

def layer_backward(stream_in, upstream, weight, cached, length):
    row_count = stream_in.shape[0]
    stream_f, inverse_rms, normed, key_heads, value_heads, query_heads, probs = layer_parts(stream_in, weight, cached, length)
    probs_low = probs.astype(jnp.bfloat16)
    upstream_heads = upstream.reshape(row_count, KV_HEADS, HEADS // KV_HEADS, HD).astype(jnp.float32)
    grad_prob = jnp.einsum('qhgd,khd->hgqk', upstream_heads, value_heads.astype(jnp.float32))
    grad_score = probs * (grad_prob - lax.optimization_barrier(jnp.sum(probs * grad_prob, axis=-1, keepdims=True)))
    grad_score = (grad_score * HD ** (-0.5)).astype(jnp.bfloat16)
    grad_query = jnp.einsum('hgqk,khd->qhgd', grad_score.astype(jnp.float32), key_heads.astype(jnp.float32)).reshape(row_count, D)
    key_count = key_heads.shape[0]
    grad_key = jnp.einsum('hgqk,qhgd->khd', grad_score.astype(jnp.float32), query_heads.astype(jnp.float32)).reshape(key_count, KV_HEADS * HD)
    grad_value = jnp.einsum('hgqk,qhgd->khd', probs_low.astype(jnp.float32), upstream_heads).reshape(key_count, KV_HEADS * HD)
    grad_rows = jnp.concatenate([grad_key, grad_value], axis=1)[PAST:].astype(jnp.bfloat16)
    grad_norm = grad_query + lax.dot_general(grad_rows, weight, (((1,), (1,)), ((), ())), preferred_element_type=jnp.float32)
    scaled = stream_f * inverse_rms
    grad_in = upstream.astype(jnp.float32) + inverse_rms * (grad_norm - scaled * lax.optimization_barrier(jnp.mean(grad_norm * scaled, axis=-1, keepdims=True)))
    return (grad_in.astype(jnp.bfloat16), normed, grad_rows)

def reference(tokens, kv_weight, cache_kv, cached_len, cotangent):
    stream = tokens
    inputs = []
    outputs = []
    for layer_at in range(LAYERS):
        weight = kv_weight[layer_at]

        def forward_doc(item_args, weight=weight):
            return layer_forward(item_args[0], weight, item_args[1], item_args[2])
        inputs.append(stream)
        stream = lax.map(forward_doc, (stream, cache_kv[layer_at], cached_len))
        outputs.append(stream)
    upstream = cotangent
    grads = []
    streams = []
    for layer_at in reversed(range(LAYERS)):
        weight = kv_weight[layer_at]

        def backward_doc(item_args, weight=weight):
            return layer_backward(item_args[0], item_args[1], weight, item_args[2], item_args[3])
        grad_in, normed, grad_rows = lax.map(backward_doc, (inputs[layer_at], upstream, cache_kv[layer_at], cached_len))
        total_grad = jnp.dot(normed.reshape(-1, D).T, grad_rows.reshape(-1, 2 * KVW), preferred_element_type=jnp.float32)
        grads.insert(0, total_grad)
        streams.insert(0, grad_in)
        upstream = grad_in
    return (jnp.stack(outputs), jnp.stack(streams), jnp.stack(grads))
```

```python
import functools

import jax
import jax.numpy as jnp
from jax import lax
from jax.experimental import pallas as pl
from jax.experimental.pallas import tpu as pltpu
from jax.sharding import PartitionSpec as P

HEADS = 32
KV_HEADS = 4
GROUP = HEADS // KV_HEADS
HD = 128
EPS = 1e-06
SCALE = HD ** (-0.5)
BF = jnp.bfloat16
F32 = jnp.float32
ANY = pl.BlockSpec(memory_space=pl.ANY)
VMEM = pl.BlockSpec(memory_space=pltpu.VMEM)
SMEM = pl.BlockSpec(memory_space=pltpu.SMEM)
TILE = 256
SPANS = 4


def dot_last(a, b):
    return lax.dot_general(a, b, (((1,), (1,)), ((), ())), preferred_element_type=F32)


def dot_first(a, b):
    return lax.dot_general(a, b, (((0,), (0,)), ((), ())), preferred_element_type=F32)


def stack_heads(ref, group, rows):
    return jnp.concatenate(
        [ref[:, pl.ds((group * GROUP + h) * HD, HD)] for h in range(GROUP)], axis=0
    )


def forward_kernel(
    rows, info, incoming, tokens, weight, cached, kv_in, saved_in0, saved_out0, probs0,
    out, kv_out, saved_in, saved_out, probs, x_buf, normed, p_buf, kv_store, sems,
):
    block = info[0]

    @pl.when(info[1] == 1)
    def _():
        at = pl.multiple_of(block * rows, rows)
        get_kv = pltpu.make_async_copy(kv_in, kv_store, sems.at[4])
        get_kv.start()

        @pl.when(info[2] == 1)
        def _():
            copy = pltpu.make_async_copy(tokens.at[pl.ds(at, rows)], x_buf, sems.at[0])
            copy.start()
            copy.wait()

        @pl.when(info[2] == 0)
        def _():
            copy = pltpu.make_async_copy(incoming, x_buf, sems.at[0])
            copy.start()
            copy.wait()

        keep_in = pltpu.make_async_copy(x_buf, saved_in.at[pl.ds(at, rows)], sems.at[1])
        keep_in.start()

        x = x_buf[...].astype(F32)
        inv = lax.rsqrt(jnp.mean(x * x, axis=-1, keepdims=True) + EPS)
        normed[...] = (x * inv).astype(BF)
        get_kv.wait()

        @pl.when(block == 0)
        def _():
            kv_store[...] = jnp.zeros_like(kv_store)

        for j in range(weight.shape[1] // TILE):
            cols = pl.ds(j * TILE, TILE)
            kv_store[pl.ds(at, rows), cols] = jnp.dot(
                normed[...], weight[:, cols], preferred_element_type=F32
            ).astype(BF)
        keep_kv = pltpu.make_async_copy(
            kv_store.at[pl.ds(at, rows)], kv_out.at[pl.ds(at, rows)], sems.at[4]
        )
        keep_kv.start()
        past = cached.shape[0]
        total = past + kv_store.shape[0]
        half = KV_HEADS * HD
        q_at = at + lax.broadcasted_iota(jnp.int32, (rows, total), 0)
        k_at = lax.broadcasted_iota(jnp.int32, (rows, total), 1)
        allowed = jnp.logical_or(
            k_at < info[3], jnp.logical_and(k_at >= past, k_at - past <= q_at)
        )
        bias = jnp.where(allowed, 0.0, -1e30)
        bias = jnp.concatenate([bias] * GROUP, axis=0)
        for g in range(KV_HEADS):
            k_cols = pl.ds(g * HD, HD)
            v_cols = pl.ds(half + g * HD, HD)
            keys = jnp.concatenate([cached[:, k_cols], kv_store[:, k_cols]], axis=0)
            values = jnp.concatenate([cached[:, v_cols], kv_store[:, v_cols]], axis=0)
            query = stack_heads(normed, g, rows)
            scores = dot_last(query, keys) * SCALE + bias
            top = jnp.max(scores, axis=-1, keepdims=True)
            e = jnp.exp(scores - top)
            p = (e * (1.0 / jnp.sum(e, axis=-1, keepdims=True))).astype(BF)
            p_buf[g] = p
            mixed = jnp.dot(p, values, preferred_element_type=F32)
            for h in range(GROUP):
                cols = pl.ds((g * GROUP + h) * HD, HD)
                out[:, cols] = (
                    x_buf[:, cols].astype(F32) + mixed[h * rows : (h + 1) * rows]
                ).astype(BF)
        keep_p = pltpu.make_async_copy(p_buf, probs.at[block], sems.at[2])
        keep_p.start()
        keep_out = pltpu.make_async_copy(out, saved_out.at[pl.ds(at, rows)], sems.at[3])
        keep_out.start()
        keep_in.wait()
        keep_kv.wait()
        keep_p.wait()
        keep_out.wait()


def forward_call(rows, info, incoming, tokens, weight, cached, state):
    kv, saved_in, saved_out, probs = state
    wide = tokens.shape[1]
    like = lambda a: jax.ShapeDtypeStruct(a.shape, a.dtype)
    res = pl.pallas_call(
        functools.partial(forward_kernel, rows),
        out_shape=(
            jax.ShapeDtypeStruct((rows, wide), BF), like(kv), like(saved_in), like(saved_out), like(probs),
        ),
        in_specs=[SMEM, ANY, ANY, VMEM, VMEM, ANY, ANY, ANY, ANY],
        out_specs=(VMEM, ANY, ANY, ANY, ANY),
        scratch_shapes=[
            pltpu.VMEM((rows, wide), BF),
            pltpu.VMEM((rows, wide), BF),
            pltpu.VMEM(probs.shape[1:], BF),
            pltpu.VMEM(kv.shape, BF),
            pltpu.SemaphoreType.DMA((5,)),
        ],
        input_output_aliases={5: 1, 6: 2, 7: 3, 8: 4},
        compiler_params=pltpu.CompilerParams(vmem_limit_bytes=24 * 2**20),
        name="forward_block",
    )(info, incoming, tokens, weight, cached, kv, saved_in, saved_out, probs)
    return res[0], res[1:]


def backward_kernel(
    rows, info, incoming, cotangent, weight, cached, kv_store, saved_in, probs, acc_in, grad_in0, done0,
    out, acc, grad_in, done, up_buf, x_buf, normed, p_buf, gn, done_buf, sems,
):
    block = info[0]

    @pl.when(info[1] == 1)
    def _():
        at = pl.multiple_of(block * rows, rows)
        get_x = pltpu.make_async_copy(saved_in.at[pl.ds(at, rows)], x_buf, sems.at[1])
        get_x.start()
        get_p = pltpu.make_async_copy(probs.at[block], p_buf, sems.at[2])
        get_p.start()

        @pl.when(info[2] == 1)
        def _():
            copy = pltpu.make_async_copy(cotangent.at[pl.ds(at, rows)], up_buf, sems.at[0])
            copy.start()
            copy.wait()

        @pl.when(info[2] == 0)
        def _():
            copy = pltpu.make_async_copy(incoming, up_buf, sems.at[0])
            copy.start()
            copy.wait()

        first = info[4] == 1
        get_x.wait()
        x = x_buf[...].astype(F32)
        inv = lax.rsqrt(jnp.mean(x * x, axis=-1, keepdims=True) + EPS)
        normed[...] = (x * inv).astype(BF)
        get_p.wait()
        past = cached.shape[0]
        half = KV_HEADS * HD
        for g in range(KV_HEADS):
            k_cols = pl.ds(g * HD, HD)
            v_cols = pl.ds(half + g * HD, HD)
            keys = jnp.concatenate([cached[:, k_cols], kv_store[:, k_cols]], axis=0)
            values = jnp.concatenate([cached[:, v_cols], kv_store[:, v_cols]], axis=0)
            query = stack_heads(normed, g, rows)
            upstream = stack_heads(up_buf, g, rows)
            p_low = p_buf[g]
            p = p_low.astype(F32)
            gp = dot_last(upstream, values)
            inner = jnp.sum(p * gp, axis=-1, keepdims=True)
            ds = (p * (gp - inner) * SCALE).astype(BF)
            gq = jnp.dot(ds, keys, preferred_element_type=F32)
            for h in range(GROUP):
                gn[:, pl.ds((g * GROUP + h) * HD, HD)] = gq[h * rows : (h + 1) * rows]
            acc[:, k_cols] = jnp.where(first, 0.0, acc_in[:, k_cols]) + dot_first(ds[:, past:], query)
            acc[:, v_cols] = jnp.where(first, 0.0, acc_in[:, v_cols]) + dot_first(
                p_low[:, past:], upstream
            )
        grad_rows = acc[pl.ds(at, rows), :].astype(BF)
        done_buf[...] = grad_rows
        keep_done = pltpu.make_async_copy(done_buf, done.at[pl.ds(at, rows)], sems.at[1])
        keep_done.start()
        inner = jnp.zeros((rows, 1), F32)
        step = 512
        for j in range(weight.shape[0] // step):
            cols = pl.ds(j * step, step)
            part = gn[:, cols] + dot_last(grad_rows, weight[cols, :])
            gn[:, cols] = part
            inner += jnp.sum(part * (x_buf[:, cols].astype(F32) * inv), axis=-1, keepdims=True)
        inner = inner * (1.0 / weight.shape[0])
        out[...] = (
            up_buf[...].astype(F32) + inv * (gn[...] - (x_buf[...].astype(F32) * inv) * inner)
        ).astype(BF)
        keep = pltpu.make_async_copy(out, grad_in.at[pl.ds(at, rows)], sems.at[3])
        keep.start()
        keep_done.wait()
        keep.wait()


def backward_call(rows, info, incoming, cotangent, weight, cached, kv, saved_in, probs, state):
    acc, grad_in, done = state
    wide = cotangent.shape[1]
    like = lambda a: jax.ShapeDtypeStruct(a.shape, a.dtype)
    res = pl.pallas_call(
        functools.partial(backward_kernel, rows),
        out_shape=(jax.ShapeDtypeStruct((rows, wide), BF), like(acc), like(grad_in), like(done)),
        in_specs=[SMEM, ANY, ANY, VMEM, VMEM, VMEM, ANY, ANY, VMEM, ANY, ANY],
        out_specs=(VMEM, VMEM, ANY, ANY),
        scratch_shapes=[
            pltpu.VMEM((rows, wide), BF),
            pltpu.VMEM((rows, wide), BF),
            pltpu.VMEM((rows, wide), BF),
            pltpu.VMEM(probs.shape[1:], BF),
            pltpu.VMEM((rows, wide), F32),
            pltpu.VMEM((rows, done.shape[1]), BF),
            pltpu.SemaphoreType.DMA((4,)),
        ],
        input_output_aliases={8: 1, 9: 2, 10: 3},
        compiler_params=pltpu.CompilerParams(vmem_limit_bytes=24 * 2**20),
        name="backward_block",
    )(info, incoming, cotangent, weight, cached, kv, saved_in, probs, acc, grad_in, done)
    return res[0], res[1:]


def hop(value, by, active):
    pairs = [(i, i + by) for i in active]
    return lax.ppermute(value, "section", pairs)


def body(tokens, kv_weight, cache_kv, cached_len, cotangent):
    at = lax.axis_index("section")
    sections = lax.axis_size("section")
    weight = kv_weight[0]
    cached = cache_kv[0, 0]
    length = cached_len[0]
    stream = tokens[0]
    upstream = cotangent[0]
    total, wide = stream.shape
    rows = total // SPANS
    ticks = sections + SPANS - 1

    def info_of(block, active, first, fresh):
        return jnp.stack(
            [jnp.clip(block, 0, SPANS - 1), active, first, length, fresh]
        ).astype(jnp.int32)

    state = (
        jnp.zeros((total, weight.shape[1]), BF),
        jnp.zeros((total, wide), BF),
        jnp.zeros((total, wide), BF),
        jnp.zeros((SPANS, KV_HEADS, GROUP * rows, cached.shape[0] + total), BF),
    )
    incoming = jnp.zeros((rows, wide), BF)
    for tick in range(ticks):
        block = tick - at
        active = jnp.logical_and(block >= 0, block < SPANS)
        info = info_of(block, active, at == 0, block == 0)
        block_out, state = forward_call(rows, info, incoming, stream, weight, cached, state)
        busy = [s for s in range(sections - 1) if 0 <= tick - s < SPANS]
        if busy:
            incoming = hop(block_out, 1, busy)
    kv, saved_in, saved_out, probs = state

    normed = normalized(saved_in)
    columns = lax.all_to_all(normed, "dp", 1, 0, tiled=True)

    back = (
        jnp.zeros((total, weight.shape[1]), F32),
        jnp.zeros((total, wide), BF),
        jnp.zeros((total, weight.shape[1]), BF),
    )
    incoming = jnp.zeros((rows, wide), BF)
    for tick in range(ticks):
        turn = tick - (sections - 1 - at)
        active = jnp.logical_and(turn >= 0, turn < SPANS)
        info = info_of(SPANS - 1 - turn, active, at == sections - 1, turn == 0)
        block_grad, back = backward_call(
            rows, info, incoming, upstream, weight, cached, kv, saved_in, probs, back
        )
        busy = [s for s in range(1, sections) if 0 <= tick - (sections - 1 - s) < SPANS]
        if busy:
            incoming = hop(block_grad, -1, busy)
    _, grad_in, done = back
    all_rows = lax.all_gather(done, "dp", axis=0, tiled=True)
    share = dot_first(columns, all_rows)
    return (saved_out[None, None], grad_in[None, None], share[None])


def normalized(stream_in):
    x = stream_in.astype(F32)
    inv = lax.rsqrt(jnp.mean(x * x, axis=-1, keepdims=True) + EPS)
    return (x * inv).astype(BF)


def solution(mesh):
    return jax.shard_map(
        body,
        mesh=mesh,
        in_specs=(
            P("dp", None, None),
            P("section", None, None),
            P("section", "dp", None, None),
            P("dp"),
            P("dp", None, None),
        ),
        out_specs=(
            P("section", "dp", None, None),
            P("section", "dp", None, None),
            P("section", "dp", None),
        ),
        check_vma=False,
    )
```

```python
import functools

import jax
import jax.numpy as jnp
from jax import lax
from jax.experimental import pallas as pl
from jax.experimental.pallas import tpu as pltpu
from jax.sharding import PartitionSpec as P

HEADS = 32
KV_HEADS = 4
GROUP = HEADS // KV_HEADS
HD = 128
EPS = 1e-06
SCALE = HD ** (-0.5)
BF = jnp.bfloat16
F32 = jnp.float32
ANY = pl.BlockSpec(memory_space=pl.ANY)
VMEM = pl.BlockSpec(memory_space=pltpu.VMEM)
SMEM = pl.BlockSpec(memory_space=pltpu.SMEM)
TILE = 256
SPANS = 4


def dot_last(a, b):
    return lax.dot_general(a, b, (((1,), (1,)), ((), ())), preferred_element_type=F32)


def dot_first(a, b):
    return lax.dot_general(a, b, (((0,), (0,)), ((), ())), preferred_element_type=F32)


def stack_heads(ref, group, rows):
    return jnp.concatenate(
        [ref[:, pl.ds((group * GROUP + h) * HD, HD)] for h in range(GROUP)], axis=0
    )


def in_hbm(a):
    return pltpu.with_memory_space_constraint(a, pltpu.HBM)


def in_vmem(a):
    return pltpu.with_memory_space_constraint(a, pltpu.VMEM)


def load_kernel(weight_in, cached_in, weight, cached, sems):
    first = pltpu.make_async_copy(weight_in, weight, sems.at[0])
    second = pltpu.make_async_copy(cached_in, cached, sems.at[1])
    first.start()
    second.start()
    first.wait()
    second.wait()


def load_call(weight, cached):
    return pl.pallas_call(
        load_kernel,
        out_shape=(pltpu.VMEM(weight.shape, BF), pltpu.VMEM(cached.shape, BF)),
        in_specs=[ANY, ANY],
        out_specs=(VMEM, VMEM),
        scratch_shapes=[pltpu.SemaphoreType.DMA((2,))],
        compiler_params=pltpu.CompilerParams(vmem_limit_bytes=24 * 2**20),
        name="load_weight",
    )(in_hbm(weight), in_hbm(cached))


def forward_kernel(
    rows, info, incoming, tokens, weight, cached, kv_in, saved_in0, saved_out0, probs0,
    out, kv_out, saved_in, saved_out, probs, x_buf, normed, p_buf, kv_store, sems,
):
    block = info[0]

    @pl.when(info[1] == 1)
    def _():
        at = pl.multiple_of(block * rows, rows)
        get_kv = pltpu.make_async_copy(kv_in, kv_store, sems.at[4])
        get_kv.start()

        @pl.when(info[2] == 1)
        def _():
            copy = pltpu.make_async_copy(tokens.at[pl.ds(at, rows)], x_buf, sems.at[0])
            copy.start()
            copy.wait()

        @pl.when(info[2] == 0)
        def _():
            copy = pltpu.make_async_copy(incoming, x_buf, sems.at[0])
            copy.start()
            copy.wait()

        keep_in = pltpu.make_async_copy(x_buf, saved_in.at[pl.ds(at, rows)], sems.at[1])
        keep_in.start()

        x = x_buf[...].astype(F32)
        inv = lax.rsqrt(jnp.mean(x * x, axis=-1, keepdims=True) + EPS)
        normed[...] = (x * inv).astype(BF)
        get_kv.wait()

        @pl.when(block == 0)
        def _():
            kv_store[...] = jnp.zeros_like(kv_store)

        for j in range(weight.shape[1] // TILE):
            cols = pl.ds(j * TILE, TILE)
            kv_store[pl.ds(at, rows), cols] = jnp.dot(
                normed[...], weight[:, cols], preferred_element_type=F32
            ).astype(BF)
        keep_kv = pltpu.make_async_copy(
            kv_store.at[pl.ds(at, rows)], kv_out.at[pl.ds(at, rows)], sems.at[4]
        )
        keep_kv.start()
        past = cached.shape[0]
        total = past + kv_store.shape[0]
        half = KV_HEADS * HD
        q_at = at + lax.broadcasted_iota(jnp.int32, (rows, total), 0)
        k_at = lax.broadcasted_iota(jnp.int32, (rows, total), 1)
        allowed = jnp.logical_or(
            k_at < info[3], jnp.logical_and(k_at >= past, k_at - past <= q_at)
        )
        bias = jnp.where(allowed, 0.0, -1e30)
        bias = jnp.concatenate([bias] * GROUP, axis=0)
        for g in range(KV_HEADS):
            k_cols = pl.ds(g * HD, HD)
            v_cols = pl.ds(half + g * HD, HD)
            keys = jnp.concatenate([cached[:, k_cols], kv_store[:, k_cols]], axis=0)
            values = jnp.concatenate([cached[:, v_cols], kv_store[:, v_cols]], axis=0)
            query = stack_heads(normed, g, rows)
            scores = dot_last(query, keys) * SCALE + bias
            top = jnp.max(scores, axis=-1, keepdims=True)
            e = jnp.exp(scores - top)
            p = (e * (1.0 / jnp.sum(e, axis=-1, keepdims=True))).astype(BF)
            p_buf[g] = p
            mixed = jnp.dot(p, values, preferred_element_type=F32)
            for h in range(GROUP):
                cols = pl.ds((g * GROUP + h) * HD, HD)
                out[:, cols] = (
                    x_buf[:, cols].astype(F32) + mixed[h * rows : (h + 1) * rows]
                ).astype(BF)
        keep_p = pltpu.make_async_copy(p_buf, probs.at[block], sems.at[2])
        keep_p.start()
        keep_out = pltpu.make_async_copy(out, saved_out.at[pl.ds(at, rows)], sems.at[3])
        keep_out.start()
        keep_in.wait()
        keep_kv.wait()
        keep_p.wait()
        keep_out.wait()


def forward_call(rows, info, incoming, tokens, weight, cached, state):
    kv, saved_in, saved_out, probs = state
    wide = tokens.shape[1]
    res = pl.pallas_call(
        functools.partial(forward_kernel, rows),
        out_shape=(
            jax.ShapeDtypeStruct((rows, wide), BF),
            pltpu.VMEM(kv.shape, BF),
            pltpu.HBM(saved_in.shape, BF),
            pltpu.HBM(saved_out.shape, BF),
            pltpu.HBM(probs.shape, BF),
        ),
        in_specs=[SMEM, ANY, ANY, VMEM, VMEM, ANY, ANY, ANY, ANY],
        out_specs=(VMEM, ANY, ANY, ANY, ANY),
        scratch_shapes=[
            pltpu.VMEM((rows, wide), BF),
            pltpu.VMEM((rows, wide), BF),
            pltpu.VMEM(probs.shape[1:], BF),
            pltpu.VMEM(kv.shape, BF),
            pltpu.SemaphoreType.DMA((5,)),
        ],
        input_output_aliases={5: 1, 6: 2, 7: 3, 8: 4},
        compiler_params=pltpu.CompilerParams(vmem_limit_bytes=24 * 2**20),
        name="forward_block",
    )(
        info, incoming, in_hbm(tokens), in_vmem(weight), in_vmem(cached), in_vmem(kv),
        in_hbm(saved_in), in_hbm(saved_out), in_hbm(probs),
    )
    return res[0], res[1:]


def backward_kernel(
    rows, info, incoming, cotangent, weight, cached, kv_store, saved_in, probs, acc_in, grad_in0, done0,
    out, acc, grad_in, done, up_buf, x_buf, normed, p_buf, gn, done_buf, sems,
):
    block = info[0]

    @pl.when(info[1] == 1)
    def _():
        at = pl.multiple_of(block * rows, rows)
        get_x = pltpu.make_async_copy(saved_in.at[pl.ds(at, rows)], x_buf, sems.at[1])
        get_x.start()
        get_p = pltpu.make_async_copy(probs.at[block], p_buf, sems.at[2])
        get_p.start()

        @pl.when(info[2] == 1)
        def _():
            copy = pltpu.make_async_copy(cotangent.at[pl.ds(at, rows)], up_buf, sems.at[0])
            copy.start()
            copy.wait()

        @pl.when(info[2] == 0)
        def _():
            copy = pltpu.make_async_copy(incoming, up_buf, sems.at[0])
            copy.start()
            copy.wait()

        first = info[4] == 1
        get_x.wait()
        x = x_buf[...].astype(F32)
        inv = lax.rsqrt(jnp.mean(x * x, axis=-1, keepdims=True) + EPS)
        normed[...] = (x * inv).astype(BF)
        get_p.wait()
        past = cached.shape[0]
        half = KV_HEADS * HD
        for g in range(KV_HEADS):
            k_cols = pl.ds(g * HD, HD)
            v_cols = pl.ds(half + g * HD, HD)
            keys = jnp.concatenate([cached[:, k_cols], kv_store[:, k_cols]], axis=0)
            values = jnp.concatenate([cached[:, v_cols], kv_store[:, v_cols]], axis=0)
            query = stack_heads(normed, g, rows)
            upstream = stack_heads(up_buf, g, rows)
            p_low = p_buf[g]
            p = p_low.astype(F32)
            gp = dot_last(upstream, values)
            inner = jnp.sum(p * gp, axis=-1, keepdims=True)
            ds = (p * (gp - inner) * SCALE).astype(BF)
            gq = jnp.dot(ds, keys, preferred_element_type=F32)
            for h in range(GROUP):
                gn[:, pl.ds((g * GROUP + h) * HD, HD)] = gq[h * rows : (h + 1) * rows]
            acc[:, k_cols] = jnp.where(first, 0.0, acc_in[:, k_cols]) + dot_first(ds[:, past:], query)
            acc[:, v_cols] = jnp.where(first, 0.0, acc_in[:, v_cols]) + dot_first(
                p_low[:, past:], upstream
            )
        grad_rows = acc[pl.ds(at, rows), :].astype(BF)
        done_buf[...] = grad_rows
        keep_done = pltpu.make_async_copy(done_buf, done.at[pl.ds(at, rows)], sems.at[1])
        keep_done.start()
        inner = jnp.zeros((rows, 1), F32)
        step = 512
        for j in range(weight.shape[0] // step):
            cols = pl.ds(j * step, step)
            part = gn[:, cols] + dot_last(grad_rows, weight[cols, :])
            gn[:, cols] = part
            inner += jnp.sum(part * (x_buf[:, cols].astype(F32) * inv), axis=-1, keepdims=True)
        inner = inner * (1.0 / weight.shape[0])
        out[...] = (
            up_buf[...].astype(F32) + inv * (gn[...] - (x_buf[...].astype(F32) * inv) * inner)
        ).astype(BF)
        keep = pltpu.make_async_copy(out, grad_in.at[pl.ds(at, rows)], sems.at[3])
        keep.start()
        keep_done.wait()
        keep.wait()


def backward_call(rows, info, incoming, cotangent, weight, cached, kv, saved_in, probs, state):
    acc, grad_in, done = state
    wide = cotangent.shape[1]
    res = pl.pallas_call(
        functools.partial(backward_kernel, rows),
        out_shape=(
            jax.ShapeDtypeStruct((rows, wide), BF),
            pltpu.VMEM(acc.shape, F32),
            pltpu.HBM(grad_in.shape, BF),
            pltpu.HBM(done.shape, BF),
        ),
        in_specs=[SMEM, ANY, ANY, VMEM, VMEM, VMEM, ANY, ANY, VMEM, ANY, ANY],
        out_specs=(VMEM, VMEM, ANY, ANY),
        scratch_shapes=[
            pltpu.VMEM((rows, wide), BF),
            pltpu.VMEM((rows, wide), BF),
            pltpu.VMEM((rows, wide), BF),
            pltpu.VMEM(probs.shape[1:], BF),
            pltpu.VMEM((rows, wide), F32),
            pltpu.VMEM((rows, done.shape[1]), BF),
            pltpu.SemaphoreType.DMA((4,)),
        ],
        input_output_aliases={8: 1, 9: 2, 10: 3},
        compiler_params=pltpu.CompilerParams(vmem_limit_bytes=24 * 2**20),
        name="backward_block",
    )(
        info, incoming, in_hbm(cotangent), in_vmem(weight), in_vmem(cached), in_vmem(kv),
        in_hbm(saved_in), in_hbm(probs), in_vmem(acc), in_hbm(grad_in), in_hbm(done),
    )
    return res[0], res[1:]


def hop(value, by, active):
    pairs = [(i, i + by) for i in active]
    return lax.ppermute(value, "section", pairs)


YS, XS, CORES = 4, 4, 2


def place(y, x, core):
    return ((y % YS) * XS + x % XS) * CORES + core % CORES


def from_offset(value, dy, dx, dcore):
    pairs = [
        (place(y + dy, x + dx, c + dcore), place(y, x, c))
        for y in range(YS)
        for x in range(XS)
        for c in range(CORES)
    ]
    return lax.ppermute(value, "dp", pairs)


def gather_near(value):
    row = jnp.stack([value] + [from_offset(value, 0, d, 0) for d in range(1, XS)])
    plane = jnp.stack([row] + [from_offset(row, d, 0, 0) for d in range(1, YS)])
    other = from_offset(plane, 0, 0, 1)
    return jnp.stack([plane, other])


def rolled(value, axis, by):
    size = value.shape[axis]
    twice = jnp.concatenate([value, value], axis=axis)
    return lax.dynamic_slice_in_dim(twice, by, size, axis)


def near_order(columns):
    docs, rows, width = columns.shape
    at = lax.axis_index("dp")
    by_place = columns.reshape(YS, XS, CORES, rows, width)
    by_place = rolled(by_place, 0, at // (XS * CORES))
    by_place = rolled(by_place, 1, (at // CORES) % XS)
    by_place = rolled(by_place, 2, at % CORES)
    return by_place.transpose(2, 0, 1, 3, 4).reshape(docs, rows, width)


def exchange(normed):
    return lax.all_to_all(normed, "dp", 1, 0, tiled=True)


def body(tokens, kv_weight, cache_kv, cached_len, cotangent):
    at = lax.axis_index("section")
    sections = lax.axis_size("section")
    docs = lax.axis_size("dp")
    weight, cached = load_call(kv_weight[0], cache_kv[0, 0])
    length = cached_len[0]
    stream = tokens[0]
    upstream = cotangent[0]
    total, wide = stream.shape
    rows = total // SPANS
    ticks = sections + SPANS - 1

    def info_of(block, active, first, fresh):
        return jnp.stack(
            [jnp.clip(block, 0, SPANS - 1), active, first, length, fresh]
        ).astype(jnp.int32)

    state = (
        jnp.zeros((total, weight.shape[1]), BF),
        jnp.zeros((total, wide), BF),
        jnp.zeros((total, wide), BF),
        jnp.zeros((SPANS, KV_HEADS, GROUP * rows, cached.shape[0] + total), BF),
    )
    incoming = jnp.zeros((rows, wide), BF)
    for tick in range(ticks):
        block = tick - at
        active = jnp.logical_and(block >= 0, block < SPANS)
        info = info_of(block, active, at == 0, block == 0)
        block_out, state = forward_call(rows, info, incoming, stream, weight, cached, state)
        busy = [s for s in range(sections - 1) if 0 <= tick - s < SPANS]
        if busy:
            incoming = hop(block_out, 1, busy)
    kv, saved_in, saved_out, probs = state

    def columns_of(rows_in):
        return exchange(normalized(rows_in))

    columns = lax.cond(
        at < sections - 1,
        columns_of,
        lambda rows_in: jnp.zeros((docs * total, wide // docs), BF),
        saved_in,
    )
    columns, saved_in, kv = lax.optimization_barrier((columns, saved_in, kv))

    back = (
        jnp.zeros((total, weight.shape[1]), F32),
        jnp.zeros((total, wide), BF),
        jnp.zeros((total, weight.shape[1]), BF),
    )
    incoming = jnp.zeros((rows, wide), BF)
    early_from = total // 2
    for tick in range(ticks):
        turn = tick - (sections - 1 - at)
        active = jnp.logical_and(turn >= 0, turn < SPANS)
        info = info_of(SPANS - 1 - turn, active, at == sections - 1, turn == 0)
        block_grad, back = backward_call(
            rows, info, incoming, upstream, weight, cached, kv, saved_in, probs, back
        )
        busy = [s for s in range(1, sections) if 0 <= tick - (sections - 1 - s) < SPANS]
        if busy:
            incoming = hop(block_grad, -1, busy)
        if tick == sections - 1 + SPANS // 2 - 1:
            early = lax.all_gather(back[2][early_from:], "dp", axis=0, tiled=True)
    _, grad_in, done = back
    columns = lax.cond(at == sections - 1, columns_of, lambda rows_in: columns, saved_in)
    columns = columns.reshape(docs, total, wide // docs)
    late_columns = near_order(columns[:, :early_from]).reshape(-1, wide // docs)
    early_columns = columns[:, early_from:].reshape(-1, wide // docs)
    late = gather_near(done[:early_from]).reshape(-1, done.shape[1])
    share = dot_first(early_columns, early) + dot_first(late_columns, late)
    return (saved_out[None, None], grad_in[None, None], share[None])


def normalized(stream_in):
    x = stream_in.astype(F32)
    inv = lax.rsqrt(jnp.mean(x * x, axis=-1, keepdims=True) + EPS)
    return (x * inv).astype(BF)


def solution(mesh):
    return jax.shard_map(
        body,
        mesh=mesh,
        in_specs=(
            P("dp", None, None),
            P("section", None, None),
            P("section", "dp", None, None),
            P("dp"),
            P("dp", None, None),
        ),
        out_specs=(
            P("section", "dp", None, None),
            P("section", "dp", None, None),
            P("section", "dp", None),
        ),
        check_vma=False,
    )
```

```python
import functools

import jax
import jax.numpy as jnp
from jax import lax
from jax.experimental import pallas as pl
from jax.experimental.pallas import tpu as pltpu
from jax.sharding import PartitionSpec as P

HEADS = 32
KV_HEADS = 4
GROUP = HEADS // KV_HEADS
HD = 128
EPS = 1e-06
SCALE = HD ** (-0.5)
BF = jnp.bfloat16
F32 = jnp.float32
ANY = pl.BlockSpec(memory_space=pl.ANY)
VMEM = pl.BlockSpec(memory_space=pltpu.VMEM)
SMEM = pl.BlockSpec(memory_space=pltpu.SMEM)
TILE = 256
SPANS = 2
LIMIT = pltpu.CompilerParams(vmem_limit_bytes=24 * 2**20)


def dot_last(a, b):
    return lax.dot_general(a, b, (((1,), (1,)), ((), ())), preferred_element_type=F32)


def dot_first(a, b):
    return lax.dot_general(a, b, (((0,), (0,)), ((), ())), preferred_element_type=F32)


def in_hbm(a):
    return pltpu.with_memory_space_constraint(a, pltpu.HBM)


def in_vmem(a):
    return pltpu.with_memory_space_constraint(a, pltpu.VMEM)


def stack_heads(ref, group, rows):
    return jnp.concatenate(
        [ref[:, pl.ds((group * GROUP + h) * HD, HD)] for h in range(GROUP)], axis=0
    )


def load_kernel(count, info, *refs):
    sources, targets, sems = refs[:count], refs[count : 2 * count], refs[-1]
    copies = [pltpu.make_async_copy(sources[i], targets[i], sems.at[i]) for i in range(count)]
    for copy in copies:
        copy.start()
    for copy in copies:
        copy.wait()


def load_call(info, arrays, spare):
    count = len(arrays)
    out = [pltpu.VMEM(a.shape, a.dtype) for a in arrays] + list(spare)
    return pl.pallas_call(
        functools.partial(load_kernel, count),
        out_shape=tuple(out),
        in_specs=[SMEM] + [ANY] * count,
        out_specs=(ANY,) * len(out),
        scratch_shapes=[pltpu.SemaphoreType.DMA((count,))],
        compiler_params=LIMIT,
        name="load_weight",
    )(info, *[in_hbm(a) for a in arrays])


def export_kernel(start, source, target, sem):
    rows = target.shape[0]
    copy = pltpu.make_async_copy(source.at[pl.ds(start, rows)], target, sem)
    copy.start()
    copy.wait()


def export_call(source, start, rows):
    return pl.pallas_call(
        functools.partial(export_kernel, start),
        out_shape=pltpu.HBM((rows, source.shape[1]), source.dtype),
        in_specs=[ANY],
        out_specs=ANY,
        scratch_shapes=[pltpu.SemaphoreType.DMA],
        compiler_params=LIMIT,
        name="export_rows",
    )(in_vmem(source))


def forward_kernel(
    step, rows, fresh, info, incoming, tokens, weight, cached, kv_in, inv_in, normed_in, saved_in, probs_in,
    out, kv, inv_all, normed_all, saved, probs, x_buf, normed,
):
    turn = step - info[0]

    @pl.when(jnp.logical_and(jnp.logical_and(turn >= 0, turn < 2 * SPANS), turn % 2 == 0))
    def _():
        block = jnp.clip(turn // 2, 0, SPANS - 1)
        at = pl.multiple_of(block * rows, rows)
        mine = pl.ds(at, rows)
        block_in = incoming[...]
        if fresh:
            block_in = jnp.where(info[0] == 0, tokens[mine, :], block_in)
        x_buf[...] = block_in
        x = block_in.astype(F32)
        inv = lax.rsqrt(jnp.mean(x * x, axis=-1, keepdims=True) + EPS)
        inv_all[mine, :] = jnp.broadcast_to(inv, (rows, HD))
        low = (x * inv).astype(BF)
        normed[...] = low
        normed_all[mine, :] = low

        @pl.when(block == 0)
        def _():
            kv[...] = jnp.zeros_like(kv)

        for j in range(weight.shape[1] // TILE):
            cols = pl.ds(j * TILE, TILE)
            kv[mine, cols] = jnp.dot(
                normed[...], weight[:, cols], preferred_element_type=F32
            ).astype(BF)
        past = cached.shape[0]
        total = past + kv.shape[0]
        half = KV_HEADS * HD
        q_at = at + lax.broadcasted_iota(jnp.int32, (rows, total), 0)
        k_at = lax.broadcasted_iota(jnp.int32, (rows, total), 1)
        allowed = jnp.logical_or(
            k_at < info[1], jnp.logical_and(k_at >= past, k_at - past <= q_at)
        )
        bias = jnp.where(allowed, 0.0, -1e30)
        bias = jnp.concatenate([bias] * GROUP, axis=0)
        for g in range(KV_HEADS):
            k_cols = pl.ds(g * HD, HD)
            v_cols = pl.ds(half + g * HD, HD)
            keys = jnp.concatenate([cached[:, k_cols], kv[:, k_cols]], axis=0)
            values = jnp.concatenate([cached[:, v_cols], kv[:, v_cols]], axis=0)
            query = stack_heads(normed, g, rows)
            scores = dot_last(query, keys) * SCALE + bias
            top = jnp.max(scores, axis=-1, keepdims=True)
            e = jnp.exp(scores - top)
            p = (e * (1.0 / jnp.sum(e, axis=-1, keepdims=True))).astype(BF)
            probs[block, g] = p
            mixed = jnp.dot(p, values, preferred_element_type=F32)
            for h in range(GROUP):
                cols = pl.ds((g * GROUP + h) * HD, HD)
                sum_out = (
                    x_buf[:, cols].astype(F32) + mixed[h * rows : (h + 1) * rows]
                ).astype(BF)
                out[:, cols] = sum_out
                saved[mine, cols] = sum_out


def vmem_like(a):
    return pltpu.VMEM(a.shape, a.dtype)


def forward_call(step, rows, info, incoming, tokens, weight, cached, state):
    fresh = step <= 2 * (SPANS - 1)
    wide = weight.shape[0]
    tokens = tokens if fresh else incoming
    operands = [incoming, tokens, weight, cached, *state]
    res = pl.pallas_call(
        functools.partial(forward_kernel, step, rows, fresh),
        out_shape=(pltpu.VMEM((rows, wide), BF), *[vmem_like(a) for a in state]),
        in_specs=[SMEM] + [VMEM] * len(operands),
        out_specs=(VMEM,) * (1 + len(state)),
        scratch_shapes=[pltpu.VMEM((rows, wide), BF), pltpu.VMEM((rows, wide), BF)],
        input_output_aliases={5 + i: 1 + i for i in range(len(state))},
        compiler_params=LIMIT,
        name="forward_block",
    )(info, *[in_vmem(a) for a in operands])
    return res[0], res[1:]


def backward_kernel(
    step, rows, sections, fresh, info, incoming, cotangent, weight, cached, kv, inv_all, normed_all, probs,
    acc_in, grad_in0, done0, out, acc, grad_in, done, up_buf, gn,
):
    turn = step - (sections - 1 - info[0])

    @pl.when(jnp.logical_and(jnp.logical_and(turn >= 0, turn < 2 * SPANS), turn % 2 == 0))
    def _():
        block = jnp.clip(SPANS - 1 - turn // 2, 0, SPANS - 1)
        at = pl.multiple_of(block * rows, rows)
        mine = pl.ds(at, rows)
        block_up = incoming[...]
        if fresh:
            block_up = jnp.where(info[0] == sections - 1, cotangent[mine, :], block_up)
        up_buf[...] = block_up
        first = turn == 0
        past = cached.shape[0]
        half = KV_HEADS * HD
        for g in range(KV_HEADS):
            k_cols = pl.ds(g * HD, HD)
            v_cols = pl.ds(half + g * HD, HD)
            keys = jnp.concatenate([cached[:, k_cols], kv[:, k_cols]], axis=0)
            values = jnp.concatenate([cached[:, v_cols], kv[:, v_cols]], axis=0)
            query = jnp.concatenate(
                [normed_all[mine, pl.ds((g * GROUP + h) * HD, HD)] for h in range(GROUP)], axis=0
            )
            upstream = stack_heads(up_buf, g, rows)
            gp = dot_last(upstream, values)
            p_low = probs[block, g]
            p = p_low.astype(F32)
            inner = jnp.sum(p * gp, axis=-1, keepdims=True)
            ds = (p * (gp - inner) * SCALE).astype(BF)
            gq = jnp.dot(ds, keys, preferred_element_type=F32)
            for h in range(GROUP):
                gn[:, pl.ds((g * GROUP + h) * HD, HD)] = gq[h * rows : (h + 1) * rows]
            acc[:, k_cols] = jnp.where(first, 0.0, acc_in[:, k_cols]) + dot_first(
                ds[:, past:], query
            )
            acc[:, v_cols] = jnp.where(first, 0.0, acc_in[:, v_cols]) + dot_first(
                p_low[:, past:], upstream
            )
        grad_rows = acc[mine, :].astype(BF)
        done[mine, :] = grad_rows
        inner = jnp.zeros((rows, HD), F32)
        width = 512
        for j in range(weight.shape[0] // width):
            cols = pl.ds(j * width, width)
            part = gn[:, cols] + dot_last(grad_rows, weight[cols, :])
            gn[:, cols] = part
            term = part * normed_all[mine, cols].astype(F32)
            for i in range(width // HD):
                inner += term[:, i * HD : (i + 1) * HD]
        inner = jnp.sum(inner, axis=-1, keepdims=True) * (1.0 / weight.shape[0])
        inv = inv_all[mine, :][:, :1]
        grad = (
            up_buf[...].astype(F32) + inv * (gn[...] - normed_all[mine, :].astype(F32) * inner)
        ).astype(BF)
        out[...] = grad
        grad_in[mine, :] = grad


def backward_call(step, rows, sections, info, incoming, cotangent, weight, cached, kept, state):
    fresh = step <= 2 * (SPANS - 1)
    wide = weight.shape[0]
    cotangent = cotangent if fresh else incoming
    operands = [incoming, cotangent, weight, cached, *kept, *state]
    start = 1 + len(operands) - len(state)
    res = pl.pallas_call(
        functools.partial(backward_kernel, step, rows, sections, fresh),
        out_shape=(pltpu.VMEM((rows, wide), BF), *[vmem_like(a) for a in state]),
        in_specs=[SMEM] + [VMEM] * len(operands),
        out_specs=(VMEM,) * (1 + len(state)),
        scratch_shapes=[pltpu.VMEM((rows, wide), BF), pltpu.VMEM((rows, wide), F32)],
        input_output_aliases={start + i: 1 + i for i in range(len(state))},
        compiler_params=LIMIT,
        name="backward_block",
    )(info, *[in_vmem(a) for a in operands])
    return res[0], res[1:]


YS, XS, CORES = 4, 4, 2


def place(y, x, core):
    return ((y % YS) * XS + x % XS) * CORES + core % CORES


def from_offset(value, dy, dx, dcore):
    pairs = [
        (place(y + dy, x + dx, c + dcore), place(y, x, c))
        for y in range(YS)
        for x in range(XS)
        for c in range(CORES)
    ]
    return lax.ppermute(value, "dp", pairs)


def gather_near(value):
    row = jnp.stack([value] + [from_offset(value, 0, d, 0) for d in range(1, XS)])
    plane = jnp.stack([row] + [from_offset(row, d, 0, 0) for d in range(1, YS)])
    other = from_offset(plane, 0, 0, 1)
    return jnp.stack([plane, other])


def rolled(value, axis, by):
    size = value.shape[axis]
    twice = jnp.concatenate([value, value], axis=axis)
    return lax.dynamic_slice_in_dim(twice, by, size, axis)


def near_order(columns):
    docs, rows, width = columns.shape
    at = lax.axis_index("dp")
    by_place = columns.reshape(YS, XS, CORES, rows, width)
    by_place = rolled(by_place, 0, at // (XS * CORES))
    by_place = rolled(by_place, 1, (at // CORES) % XS)
    by_place = rolled(by_place, 2, at % CORES)
    return by_place.transpose(2, 0, 1, 3, 4).reshape(docs, rows, width)


def body(tokens, kv_weight, cache_kv, cached_len, cotangent):
    at = lax.axis_index("section")
    sections = lax.axis_size("section")
    docs = lax.axis_size("dp")
    total, wide = tokens.shape[1:]
    pair = kv_weight.shape[2]
    rows = total // SPANS
    past = cache_kv.shape[2]
    width = wide // docs
    steps = sections + 2 * (SPANS - 1)
    info = jnp.stack([at, cached_len[0]]).astype(jnp.int32)

    def busy(step):
        return [s for s in range(sections) if step - s in range(0, 2 * SPANS, 2)]

    weight, cached, stream, *state, incoming = load_call(
        info,
        [kv_weight[0], cache_kv[0, 0], tokens[0]],
        [
            pltpu.VMEM((total, pair), BF),
            pltpu.VMEM((total, HD), F32),
            pltpu.VMEM((total, wide), BF),
            pltpu.VMEM((total, wide), BF),
            pltpu.VMEM((SPANS, KV_HEADS, GROUP * rows, past + total), BF),
            pltpu.VMEM((rows, wide), BF),
        ],
    )
    soon = sections - 1 - 2 * (SPANS - 1)

    def columns_of(normed):
        return lax.all_to_all(normed, "dp", 1, 0, tiled=True)

    for step in range(steps):
        block_out, state = forward_call(step, rows, info, incoming, stream, weight, cached, state)
        pairs = [(s, s + 1) for s in busy(step) if s + 1 < sections]
        if pairs:
            incoming = lax.ppermute(block_out, "section", pairs)
        if step == sections - 2:
            columns = lax.cond(
                at < soon,
                columns_of,
                lambda normed: jnp.zeros((docs * total, width), BF),
                state[2],
            )
            columns, info = lax.optimization_barrier((columns, info))
            weight, cached, upstream, *back, spare_in = load_call(
                info,
                [kv_weight[0], cache_kv[0, 0], cotangent[0]],
                [
                    pltpu.VMEM((total, pair), F32),
                    pltpu.VMEM((total, wide), BF),
                    pltpu.VMEM((total, pair), BF),
                    pltpu.VMEM((rows, wide), BF),
                ],
            )
    kv, inv, normed, hidden, probs = state

    incoming = spare_in
    early_from = total // SPANS
    for step in range(steps):
        block_grad, back = backward_call(
            step, rows, sections, info, incoming, upstream, weight, cached, (kv, inv, normed, probs), back
        )
        pairs = [(sections - 1 - s, sections - 2 - s) for s in busy(step) if s + 1 < sections]
        if pairs:
            incoming = lax.ppermute(block_grad, "section", pairs)
        if step == steps - 3:
            early = export_call(back[2], early_from, total - early_from)
            early = lax.all_gather(early, "dp", axis=0, tiled=True)
    _, grad_in, done = back
    columns = lax.cond(at >= soon, columns_of, lambda normed: columns, normed)
    columns = columns.reshape(docs, total, width)
    late_columns = near_order(columns[:, :early_from]).reshape(-1, width)
    early_columns = columns[:, early_from:].reshape(-1, width)
    late = gather_near(done[:early_from]).reshape(-1, pair)
    share = dot_first(early_columns, early) + dot_first(late_columns, late)
    return (hidden[None, None], grad_in[None, None], share[None])


def solution(mesh):
    return jax.shard_map(
        body,
        mesh=mesh,
        in_specs=(
            P("dp", None, None),
            P("section", None, None),
            P("section", "dp", None, None),
            P("dp"),
            P("dp", None, None),
        ),
        out_specs=(
            P("section", "dp", None, None),
            P("section", "dp", None, None),
            P("section", "dp", None),
        ),
        check_vma=False,
    )
```

```python
import functools

import jax
import jax.numpy as jnp
from jax import lax
from jax.experimental import pallas as pl
from jax.experimental.pallas import tpu as pltpu
from jax.sharding import Mesh, PartitionSpec as P

HEADS = 32
KV_HEADS = 4
GROUP = HEADS // KV_HEADS
HD = 128
EPS = 1e-06
SCALE = HD ** (-0.5)
BF = jnp.bfloat16
F32 = jnp.float32
ANY = pl.BlockSpec(memory_space=pl.ANY)
VMEM = pl.BlockSpec(memory_space=pltpu.VMEM)
SMEM = pl.BlockSpec(memory_space=pltpu.SMEM)
TILE = 256
SPANS = 2
LIMIT = pltpu.CompilerParams(vmem_limit_bytes=24 * 2**20)


def dot_last(a, b):
    return lax.dot_general(a, b, (((1,), (1,)), ((), ())), preferred_element_type=F32)


def dot_first(a, b):
    return lax.dot_general(a, b, (((0,), (0,)), ((), ())), preferred_element_type=F32)


def in_hbm(a):
    return pltpu.with_memory_space_constraint(a, pltpu.HBM)


def in_vmem(a):
    return pltpu.with_memory_space_constraint(a, pltpu.VMEM)


def stack_heads(ref, group, rows):
    return jnp.concatenate(
        [ref[:, pl.ds((group * GROUP + h) * HD, HD)] for h in range(GROUP)], axis=0
    )


def load_kernel(count, info, *refs):
    sources, targets, sems = refs[:count], refs[count : 2 * count], refs[-1]
    copies = [pltpu.make_async_copy(sources[i], targets[i], sems.at[i]) for i in range(count)]
    for copy in copies:
        copy.start()
    for copy in copies:
        copy.wait()


def load_call(info, arrays, spare):
    count = len(arrays)
    out = [pltpu.VMEM(a.shape, a.dtype) for a in arrays] + list(spare)
    return pl.pallas_call(
        functools.partial(load_kernel, count),
        out_shape=tuple(out),
        in_specs=[SMEM] + [ANY] * count,
        out_specs=(ANY,) * len(out),
        scratch_shapes=[pltpu.SemaphoreType.DMA((count,))],
        compiler_params=LIMIT,
        name="load_weight",
    )(info, *[in_hbm(a) for a in arrays])


def forward_kernel(
    step, rows, fresh, info, incoming, tokens, weight, cached, kv_in, inv_in, normed_in, saved_in, probs_in,
    out, kv, inv_all, normed_all, saved, probs, x_buf, normed,
):
    turn = step - info[0] - info[2]

    @pl.when(jnp.logical_and(jnp.logical_and(turn >= 0, turn < 2 * SPANS), turn % 2 == 0))
    def _():
        block = jnp.clip(turn // 2, 0, SPANS - 1)
        at = pl.multiple_of(block * rows, rows)
        mine = pl.ds(at, rows)
        block_in = incoming[...]
        if fresh:
            block_in = jnp.where(info[0] == 0, tokens[mine, :], block_in)
        x_buf[...] = block_in
        x = block_in.astype(F32)
        inv = lax.rsqrt(jnp.mean(x * x, axis=-1, keepdims=True) + EPS)
        inv_all[mine, :] = jnp.broadcast_to(inv, (rows, HD))
        low = (x * inv).astype(BF)
        normed[...] = low
        normed_all[mine, :] = low

        @pl.when(block == 0)
        def _():
            kv[...] = jnp.zeros_like(kv)

        for j in range(weight.shape[1] // TILE):
            cols = pl.ds(j * TILE, TILE)
            kv[mine, cols] = jnp.dot(
                normed[...], weight[:, cols], preferred_element_type=F32
            ).astype(BF)
        past = cached.shape[0]
        total = past + kv.shape[0]
        half = KV_HEADS * HD
        q_at = at + lax.broadcasted_iota(jnp.int32, (rows, total), 0)
        k_at = lax.broadcasted_iota(jnp.int32, (rows, total), 1)
        allowed = jnp.logical_or(
            k_at < info[1], jnp.logical_and(k_at >= past, k_at - past <= q_at)
        )
        bias = jnp.where(allowed, 0.0, -1e30)
        bias = jnp.concatenate([bias] * GROUP, axis=0)
        for g in range(KV_HEADS):
            k_cols = pl.ds(g * HD, HD)
            v_cols = pl.ds(half + g * HD, HD)
            keys = jnp.concatenate([cached[:, k_cols], kv[:, k_cols]], axis=0)
            values = jnp.concatenate([cached[:, v_cols], kv[:, v_cols]], axis=0)
            query = stack_heads(normed, g, rows)
            scores = dot_last(query, keys) * SCALE + bias
            top = jnp.max(scores, axis=-1, keepdims=True)
            e = jnp.exp(scores - top)
            p = (e * (1.0 / jnp.sum(e, axis=-1, keepdims=True))).astype(BF)
            probs[block, g] = p
            mixed = jnp.dot(p, values, preferred_element_type=F32)
            for h in range(GROUP):
                cols = pl.ds((g * GROUP + h) * HD, HD)
                sum_out = (
                    x_buf[:, cols].astype(F32) + mixed[h * rows : (h + 1) * rows]
                ).astype(BF)
                out[:, cols] = sum_out
                saved[mine, cols] = sum_out


def vmem_like(a):
    return pltpu.VMEM(a.shape, a.dtype)


def forward_call(step, rows, info, incoming, tokens, weight, cached, state):
    fresh = step <= 2 * SPANS - 1
    wide = weight.shape[0]
    tokens = tokens if fresh else incoming
    operands = [incoming, tokens, weight, cached, *state]
    res = pl.pallas_call(
        functools.partial(forward_kernel, step, rows, fresh),
        out_shape=(pltpu.VMEM((rows, wide), BF), *[vmem_like(a) for a in state]),
        in_specs=[SMEM] + [VMEM] * len(operands),
        out_specs=(VMEM,) * (1 + len(state)),
        scratch_shapes=[pltpu.VMEM((rows, wide), BF), pltpu.VMEM((rows, wide), BF)],
        input_output_aliases={5 + i: 1 + i for i in range(len(state))},
        compiler_params=LIMIT,
        name="forward_block",
    )(info, *[in_vmem(a) for a in operands])
    return res[0], res[1:]


def backward_kernel(
    step, rows, sections, fresh, info, incoming, cotangent, weight, cached, kv, inv_all, normed_all, probs,
    acc_in, grad_in0, done0, out, acc, grad_in, done, up_buf, gn,
):
    turn = step - (sections - 1 - info[0]) - info[2]

    @pl.when(jnp.logical_and(jnp.logical_and(turn >= 0, turn < 2 * SPANS), turn % 2 == 0))
    def _():
        block = jnp.clip(SPANS - 1 - turn // 2, 0, SPANS - 1)
        at = pl.multiple_of(block * rows, rows)
        mine = pl.ds(at, rows)
        block_up = incoming[...]
        if fresh:
            block_up = jnp.where(info[0] == sections - 1, cotangent[mine, :], block_up)
        up_buf[...] = block_up
        first = turn == 0
        past = cached.shape[0]
        half = KV_HEADS * HD
        for g in range(KV_HEADS):
            k_cols = pl.ds(g * HD, HD)
            v_cols = pl.ds(half + g * HD, HD)
            keys = jnp.concatenate([cached[:, k_cols], kv[:, k_cols]], axis=0)
            values = jnp.concatenate([cached[:, v_cols], kv[:, v_cols]], axis=0)
            query = jnp.concatenate(
                [normed_all[mine, pl.ds((g * GROUP + h) * HD, HD)] for h in range(GROUP)], axis=0
            )
            upstream = stack_heads(up_buf, g, rows)
            gp = dot_last(upstream, values)
            p_low = probs[block, g]
            p = p_low.astype(F32)
            inner = jnp.sum(p * gp, axis=-1, keepdims=True)
            ds = (p * (gp - inner) * SCALE).astype(BF)
            gq = jnp.dot(ds, keys, preferred_element_type=F32)
            for h in range(GROUP):
                gn[:, pl.ds((g * GROUP + h) * HD, HD)] = gq[h * rows : (h + 1) * rows]
            acc[:, k_cols] = jnp.where(first, 0.0, acc_in[:, k_cols]) + dot_first(
                ds[:, past:], query
            )
            acc[:, v_cols] = jnp.where(first, 0.0, acc_in[:, v_cols]) + dot_first(
                p_low[:, past:], upstream
            )
        grad_rows = acc[mine, :].astype(BF)
        done[mine, :] = grad_rows
        inner = jnp.zeros((rows, HD), F32)
        width = 512
        for j in range(weight.shape[0] // width):
            cols = pl.ds(j * width, width)
            part = gn[:, cols] + dot_last(grad_rows, weight[cols, :])
            gn[:, cols] = part
            term = part * normed_all[mine, cols].astype(F32)
            for i in range(width // HD):
                inner += term[:, i * HD : (i + 1) * HD]
        inner = jnp.sum(inner, axis=-1, keepdims=True) * (1.0 / weight.shape[0])
        inv = inv_all[mine, :][:, :1]
        grad = (
            up_buf[...].astype(F32) + inv * (gn[...] - normed_all[mine, :].astype(F32) * inner)
        ).astype(BF)
        out[...] = grad
        grad_in[mine, :] = grad


def backward_call(step, rows, sections, info, incoming, cotangent, weight, cached, kept, state):
    fresh = step <= 2 * SPANS - 1
    wide = weight.shape[0]
    cotangent = cotangent if fresh else incoming
    operands = [incoming, cotangent, weight, cached, *kept, *state]
    start = 1 + len(operands) - len(state)
    res = pl.pallas_call(
        functools.partial(backward_kernel, step, rows, sections, fresh),
        out_shape=(pltpu.VMEM((rows, wide), BF), *[vmem_like(a) for a in state]),
        in_specs=[SMEM] + [VMEM] * len(operands),
        out_specs=(VMEM,) * (1 + len(state)),
        scratch_shapes=[pltpu.VMEM((rows, wide), BF), pltpu.VMEM((rows, wide), F32)],
        input_output_aliases={start + i: 1 + i for i in range(len(state))},
        compiler_params=LIMIT,
        name="backward_block",
    )(info, *[in_vmem(a) for a in operands])
    return res[0], res[1:]


YS, XS, CORES = 4, 4, 2


def from_offset(value, axis, by):
    size = lax.axis_size(axis)
    return lax.ppermute(value, axis, [((i + by) % size, i) for i in range(size)])


def rolled(value, axis, by):
    size = value.shape[axis]
    twice = jnp.concatenate([value, value], axis=axis)
    return lax.dynamic_slice_in_dim(twice, by, size, axis)


def columns_of(normed):
    rows, wide = normed.shape
    width = wide // (YS * XS * CORES)
    split = normed.reshape(rows, YS, XS * CORES, width).transpose(0, 2, 1, 3)
    columns = lax.all_to_all(split, ("x", "core"), 1, 0, tiled=True)
    columns = columns.reshape(XS, CORES, rows, YS, width)
    columns = rolled(columns, 0, lax.axis_index("x"))
    columns = rolled(columns, 1, lax.axis_index("core"))
    columns = rolled(columns, 3, lax.axis_index("y"))
    return columns.transpose(1, 3, 0, 2, 4).reshape(CORES, YS, XS * rows, width)


def summed_share(columns, grad_rows):
    near = [grad_rows] + [from_offset(grad_rows, "x", d) for d in range(1, XS)]
    near = jnp.concatenate(near, axis=0)
    other = from_offset(near, "core", 1)

    def part(d):
        return dot_first(columns[0, d], near) + dot_first(columns[1, d], other)

    total = None
    parts = [from_offset(part(d).astype(BF), "y", -d) for d in range(1, YS)]
    total = part(0)
    for piece in parts:
        total = total + piece.astype(F32)
    return total


def body(tokens, kv_weight, cache_kv, cached_len, cotangent):
    at = lax.axis_index("section")
    sections = lax.axis_size("section")
    total, wide = tokens.shape[1:]
    pair = kv_weight.shape[2]
    rows = total // SPANS
    past = cache_kv.shape[2]
    width = wide // (YS * XS * CORES)
    steps = sections + 2 * SPANS - 1
    info = jnp.stack([at, cached_len[0], lax.axis_index("core")]).astype(jnp.int32)

    def movers(step, by):
        lead = [s if by > 0 else sections - 1 - s for s in range(sections)]
        return [
            (s * CORES + c, (s + by) * CORES + c)
            for s in range(sections)
            for c in range(CORES)
            if step - lead[s] - c in range(0, 2 * SPANS, 2) and 0 <= s + by < sections
        ]

    def hop(value, step, by):
        pairs = movers(step, by)
        return lax.ppermute(value, ("section", "core"), pairs) if pairs else None

    weight, cached, stream, *state, incoming = load_call(
        info,
        [kv_weight[0], cache_kv[0, 0], tokens[0]],
        [
            pltpu.VMEM((total, pair), BF),
            pltpu.VMEM((total, HD), F32),
            pltpu.VMEM((total, wide), BF),
            pltpu.VMEM((total, wide), BF),
            pltpu.VMEM((SPANS, KV_HEADS, GROUP * rows, past + total), BF),
            pltpu.VMEM((rows, wide), BF),
        ],
    )
    soon = sections - 2 * SPANS

    for step in range(steps):
        block_out, state = forward_call(step, rows, info, incoming, stream, weight, cached, state)
        incoming = hop(block_out, step, 1)
        if step == sections - 2:
            columns = lax.cond(
                at < soon,
                columns_of,
                lambda normed: jnp.zeros((CORES, YS, XS * total, width), BF),
                state[2],
            )
            columns, info = lax.optimization_barrier((columns, info))
            weight, cached, upstream, *back, spare_in = load_call(
                info,
                [kv_weight[0], cache_kv[0, 0], cotangent[0]],
                [
                    pltpu.VMEM((total, pair), F32),
                    pltpu.VMEM((total, wide), BF),
                    pltpu.VMEM((total, pair), BF),
                    pltpu.VMEM((rows, wide), BF),
                ],
            )
    kv, inv, normed, hidden, probs = state

    incoming = spare_in
    for step in range(steps):
        block_grad, back = backward_call(
            step, rows, sections, info, incoming, upstream, weight, cached, (kv, inv, normed, probs), back
        )
        incoming = hop(block_grad, step, -1)
    _, grad_in, done = back
    columns = lax.cond(at >= soon, columns_of, lambda normed: columns, normed)
    share = summed_share(columns, done)
    return (hidden[None, None], grad_in[None, None], share[None])


def solution(mesh):
    devices = mesh.devices.reshape(-1, YS, XS, CORES)
    dp = ("y", "x", "core")
    return jax.shard_map(
        body,
        mesh=Mesh(devices, ("section",) + dp),
        in_specs=(
            P(dp, None, None),
            P("section", None, None),
            P("section", dp, None, None),
            P(dp),
            P(dp, None, None),
        ),
        out_specs=(
            P("section", dp, None, None),
            P("section", dp, None, None),
            P("section", dp, None),
        ),
        check_vma=False,
    )
```

```python
import functools

import jax
import jax.numpy as jnp
from jax import lax
from jax.experimental import pallas as pl
from jax.experimental.pallas import tpu as pltpu
from jax.sharding import Mesh, PartitionSpec as P

HEADS = 32
KV_HEADS = 4
GROUP = HEADS // KV_HEADS
HD = 128
EPS = 1e-06
SCALE = HD ** (-0.5)
BF = jnp.bfloat16
F32 = jnp.float32
ANY = pl.BlockSpec(memory_space=pl.ANY)
VMEM = pl.BlockSpec(memory_space=pltpu.VMEM)
SMEM = pl.BlockSpec(memory_space=pltpu.SMEM)
TILE = 512
WIDTH = 1024
SPANS = 4
LAG = 2
LIMIT = pltpu.CompilerParams(vmem_limit_bytes=24 * 2**20)


def dot_last(a, b):
    return lax.dot_general(a, b, (((1,), (1,)), ((), ())), preferred_element_type=F32)


def dot_first(a, b):
    return lax.dot_general(a, b, (((0,), (0,)), ((), ())), preferred_element_type=F32)


def in_hbm(a):
    return pltpu.with_memory_space_constraint(a, pltpu.HBM)


def in_vmem(a):
    return pltpu.with_memory_space_constraint(a, pltpu.VMEM)


def stack_heads(ref, group, rows):
    return jnp.concatenate(
        [ref[:, pl.ds((group * GROUP + h) * HD, HD)] for h in range(GROUP)], axis=0
    )


def load_kernel(count, info, *refs):
    sources, targets, sems = refs[:count], refs[count : 2 * count], refs[-1]
    copies = [pltpu.make_async_copy(sources[i], targets[i], sems.at[i]) for i in range(count)]
    for copy in copies:
        copy.start()
    for copy in copies:
        copy.wait()


def load_call(info, arrays, spare):
    count = len(arrays)
    out = [pltpu.VMEM(a.shape, a.dtype) for a in arrays] + list(spare)
    return pl.pallas_call(
        functools.partial(load_kernel, count),
        out_shape=tuple(out),
        in_specs=[SMEM] + [ANY] * count,
        out_specs=(ANY,) * len(out),
        scratch_shapes=[pltpu.SemaphoreType.DMA((count,))],
        compiler_params=LIMIT,
        name="load_weight",
    )(info, *[in_hbm(a) for a in arrays])


def forward_kernel(
    step, rows, fresh, info, incoming, tokens, weight, cached, kv_in, inv_in, normed_in, saved_in, probs_in,
    out, kv, inv_all, normed_all, saved, probs, x_buf, normed,
):
    turn = step - LAG * info[0]

    @pl.when(jnp.logical_and(turn >= 0, turn < SPANS))
    def _():
        block = jnp.clip(turn, 0, SPANS - 1)
        at = pl.multiple_of(block * rows, rows)
        mine = pl.ds(at, rows)
        block_in = incoming[...]
        if fresh:
            block_in = jnp.where(info[0] == 0, tokens[mine, :], block_in)
        x_buf[...] = block_in
        x = block_in.astype(F32)
        inv = lax.rsqrt(jnp.mean(x * x, axis=-1, keepdims=True) + EPS)
        inv_all[mine, :] = jnp.broadcast_to(inv, (rows, HD))
        low = (x * inv).astype(BF)
        normed[...] = low
        normed_all[mine, :] = low

        @pl.when(block == 0)
        def _():
            kv[...] = jnp.zeros_like(kv)

        @pl.loop(0, weight.shape[1] // TILE)
        def _(j):
            cols = pl.ds(pl.multiple_of(j * TILE, TILE), TILE)
            kv[mine, cols] = jnp.dot(
                normed[...], weight[:, cols], preferred_element_type=F32
            ).astype(BF)

        past = cached.shape[0]
        total = past + kv.shape[0]
        half = KV_HEADS * HD
        q_at = at + lax.broadcasted_iota(jnp.int32, (rows, total), 0)
        k_at = lax.broadcasted_iota(jnp.int32, (rows, total), 1)
        allowed = jnp.logical_or(
            k_at < info[1], jnp.logical_and(k_at >= past, k_at - past <= q_at)
        )
        bias = jnp.where(allowed, 0.0, -1e30)
        bias = jnp.concatenate([bias] * GROUP, axis=0)
        for g in range(KV_HEADS):
            k_cols = pl.ds(g * HD, HD)
            v_cols = pl.ds(half + g * HD, HD)
            keys = jnp.concatenate([cached[:, k_cols], kv[:, k_cols]], axis=0)
            values = jnp.concatenate([cached[:, v_cols], kv[:, v_cols]], axis=0)
            query = stack_heads(normed, g, rows)
            scores = dot_last(query, keys) * SCALE + bias
            top = jnp.max(scores, axis=-1, keepdims=True)
            e = jnp.exp(scores - top)
            p = (e * (1.0 / jnp.sum(e, axis=-1, keepdims=True))).astype(BF)
            probs[block, g] = p
            mixed = jnp.dot(p, values, preferred_element_type=F32)
            for h in range(GROUP):
                cols = pl.ds((g * GROUP + h) * HD, HD)
                sum_out = (
                    x_buf[:, cols].astype(F32) + mixed[h * rows : (h + 1) * rows]
                ).astype(BF)
                out[:, cols] = sum_out
                saved[mine, cols] = sum_out


def vmem_like(a):
    return pltpu.VMEM(a.shape, a.dtype)


def forward_call(step, rows, info, incoming, tokens, weight, cached, state):
    fresh = step < SPANS
    wide = weight.shape[0]
    tokens = tokens if fresh else incoming
    operands = [incoming, tokens, weight, cached, *state]
    res = pl.pallas_call(
        functools.partial(forward_kernel, step, rows, fresh),
        out_shape=(pltpu.VMEM((rows, wide), BF), *[vmem_like(a) for a in state]),
        in_specs=[SMEM] + [VMEM] * len(operands),
        out_specs=(VMEM,) * (1 + len(state)),
        scratch_shapes=[pltpu.VMEM((rows, wide), BF), pltpu.VMEM((rows, wide), BF)],
        input_output_aliases={5 + i: 1 + i for i in range(len(state))},
        compiler_params=LIMIT,
        name="forward_block",
    )(info, *[in_vmem(a) for a in operands])
    return res[0], res[1:]


def backward_kernel(
    step, rows, sections, fresh, info, incoming, cotangent, weight, cached, kv, inv_all, normed_all, probs,
    acc_in, grad_in0, done0, out, acc, grad_in, done, up_buf, gn,
):
    turn = step - LAG * (sections - 1 - info[0])

    @pl.when(jnp.logical_and(turn >= 0, turn < SPANS))
    def _():
        block = jnp.clip(SPANS - 1 - turn, 0, SPANS - 1)
        at = pl.multiple_of(block * rows, rows)
        mine = pl.ds(at, rows)
        block_up = incoming[...]
        if fresh:
            block_up = jnp.where(info[0] == sections - 1, cotangent[mine, :], block_up)
        up_buf[...] = block_up
        first = turn == 0
        past = cached.shape[0]
        half = KV_HEADS * HD
        for g in range(KV_HEADS):
            k_cols = pl.ds(g * HD, HD)
            v_cols = pl.ds(half + g * HD, HD)
            keys = jnp.concatenate([cached[:, k_cols], kv[:, k_cols]], axis=0)
            values = jnp.concatenate([cached[:, v_cols], kv[:, v_cols]], axis=0)
            query = jnp.concatenate(
                [normed_all[mine, pl.ds((g * GROUP + h) * HD, HD)] for h in range(GROUP)], axis=0
            )
            upstream = stack_heads(up_buf, g, rows)
            gp = dot_last(upstream, values)
            p_low = probs[block, g]
            p = p_low.astype(F32)
            inner = jnp.sum(p * gp, axis=-1, keepdims=True)
            ds = (p * (gp - inner) * SCALE).astype(BF)
            gq = jnp.dot(ds, keys, preferred_element_type=F32)
            for h in range(GROUP):
                gn[:, pl.ds((g * GROUP + h) * HD, HD)] = gq[h * rows : (h + 1) * rows]
            acc[:, k_cols] = jnp.where(first, 0.0, acc_in[:, k_cols]) + dot_first(
                ds[:, past:], query
            )
            acc[:, v_cols] = jnp.where(first, 0.0, acc_in[:, v_cols]) + dot_first(
                p_low[:, past:], upstream
            )
        grad_rows = acc[mine, :].astype(BF)
        done[mine, :] = grad_rows
        width = WIDTH

        def project(j, inner):
            cols = pl.ds(pl.multiple_of(j * width, width), width)
            part = gn[:, cols] + dot_last(grad_rows, weight[cols, :])
            gn[:, cols] = part
            term = part * normed_all[mine, cols].astype(F32)
            for i in range(width // HD):
                inner += term[:, i * HD : (i + 1) * HD]
            return inner

        inner = lax.fori_loop(0, weight.shape[0] // width, project, jnp.zeros((rows, HD), F32))
        inner = jnp.sum(inner, axis=-1, keepdims=True) * (1.0 / weight.shape[0])
        inv = inv_all[mine, :][:, :1]
        grad = (
            up_buf[...].astype(F32) + inv * (gn[...] - normed_all[mine, :].astype(F32) * inner)
        ).astype(BF)
        out[...] = grad
        grad_in[mine, :] = grad


def backward_call(step, rows, sections, info, incoming, cotangent, weight, cached, kept, state):
    fresh = step < SPANS
    wide = weight.shape[0]
    cotangent = cotangent if fresh else incoming
    operands = [incoming, cotangent, weight, cached, *kept, *state]
    start = 1 + len(operands) - len(state)
    res = pl.pallas_call(
        functools.partial(backward_kernel, step, rows, sections, fresh),
        out_shape=(pltpu.VMEM((rows, wide), BF), *[vmem_like(a) for a in state]),
        in_specs=[SMEM] + [VMEM] * len(operands),
        out_specs=(VMEM,) * (1 + len(state)),
        scratch_shapes=[pltpu.VMEM((rows, wide), BF), pltpu.VMEM((rows, wide), F32)],
        input_output_aliases={start + i: 1 + i for i in range(len(state))},
        compiler_params=LIMIT,
        name="backward_block",
    )(info, *[in_vmem(a) for a in operands])
    return res[0], res[1:]


YS, XS, CORES = 4, 4, 2


def pieces_kernel(late, info, normed, *refs):
    pieces = refs[1 + XS : 1 + 2 * XS]
    width = normed.shape[1] // (YS * XS)

    @pl.when((info[0] == info[2]) == late)
    def _():
        for k, piece in enumerate(pieces):
            x = lax.rem(info[4] + k, XS)
            for y in range(YS):
                cols = pl.ds(pl.multiple_of((y * XS + x) * width, width), width)
                piece[:, y * width : (y + 1) * width] = normed[:, cols]


def pieces_call(late, info, normed, pieces, done):
    *pieces, done = pl.pallas_call(
        functools.partial(pieces_kernel, late),
        out_shape=tuple(vmem_like(a) for a in (*pieces, done)),
        in_specs=[SMEM] + [VMEM] * (2 + XS),
        out_specs=(VMEM,) * (1 + XS),
        input_output_aliases={2 + i: i for i in range(1 + XS)},
        compiler_params=LIMIT,
        name="column_pieces",
    )(info, in_vmem(normed), *[in_vmem(a) for a in pieces], in_vmem(done))
    return pieces, done


def product_kernel(info, *refs):
    columns, grads = refs[:XS], refs[XS : 2 * XS]
    away, mine, left, right = refs[2 * XS :]
    rows, width = columns[0].shape[0], columns[0].shape[1] // (YS * CORES)
    for d in range(XS):
        left[pl.ds(d * rows, rows), :] = columns[d][...]
        right[pl.ds(d * rows, rows), :] = grads[d][...]

    @pl.loop(0, YS)
    def _(j):
        y = lax.rem(info[3] + j, YS)
        for core in range(CORES):
            whose = jnp.where(core == 0, 1 - info[5], info[5])
            cols = pl.ds(pl.multiple_of((y * CORES + whose) * width, width), width)
            part = dot_first(left[:, cols], right[...])
            if core == 0:
                away[j] = part.astype(BF)
            else:
                mine[j] = part


def product_call(info, columns, grads):
    rows, pair = grads[0].shape
    width = columns[0].shape[1] // (YS * CORES)
    return pl.pallas_call(
        product_kernel,
        out_shape=(pltpu.VMEM((YS, width, pair), BF), pltpu.VMEM((YS, width, pair), F32)),
        in_specs=[SMEM] + [VMEM] * (2 * XS),
        out_specs=(VMEM, VMEM),
        scratch_shapes=[
            pltpu.VMEM((XS * rows, columns[0].shape[1]), BF),
            pltpu.VMEM((XS * rows, pair), BF),
        ],
        compiler_params=LIMIT,
        name="document_product",
    )(info, *[in_vmem(a) for a in columns], *[in_vmem(a) for a in grads])


def merge_kernel(mine, other, *parts):
    parts[0][...] = mine[0] + other[0].astype(F32)
    for j in range(1, YS):
        parts[j][...] = (mine[j] + other[j].astype(F32)).astype(BF)


def merge_call(mine, other):
    shape = mine.shape[1:]
    return pl.pallas_call(
        merge_kernel,
        out_shape=tuple(pltpu.VMEM(shape, F32 if j == 0 else BF) for j in range(YS)),
        in_specs=[VMEM, VMEM],
        out_specs=(VMEM,) * YS,
        compiler_params=LIMIT,
        name="merge_cores",
    )(in_vmem(mine), in_vmem(other))


def from_offset(value, axis, by):
    size = lax.axis_size(axis)
    return lax.ppermute(value, axis, [((i + by) % size, i) for i in range(size)])


def summed_share(info, pieces, grad_rows):
    grads = [grad_rows] + [from_offset(grad_rows, "x", d) for d in range(1, XS)]
    columns = [pieces[0]] + [from_offset(pieces[XS - d], "x", d) for d in range(1, XS)]
    away, mine = product_call(info, columns, grads)
    total, *parts = merge_call(mine, from_offset(away, "core", 1))
    for j, part in enumerate(parts, 1):
        total = total + from_offset(part, "y", -j).astype(F32)
    return total


def body(tokens, kv_weight, cache_kv, cached_len, cotangent):
    at = lax.axis_index("section")
    sections = lax.axis_size("section")
    total, wide = tokens.shape[1:]
    pair = kv_weight.shape[2]
    rows = total // SPANS
    past = cache_kv.shape[2]
    steps = LAG * (sections - 1) + SPANS
    where = [lax.axis_index(axis) for axis in ("y", "x", "core")]
    info = jnp.stack([at, cached_len[0], sections - 1, *where]).astype(jnp.int32)

    def hop(value, step, by):
        movers = [
            (s, s + by)
            for s in range(sections)
            if 0 <= step - LAG * (s if by > 0 else sections - 1 - s) < SPANS and 0 <= s + by < sections
        ]
        return lax.ppermute(value, "section", movers) if movers else None

    weight, cached, stream, upstream, *spare = load_call(
        info,
        [kv_weight[0], cache_kv[0, 0], tokens[0], cotangent[0]],
        [
            pltpu.VMEM((total, pair), BF),
            pltpu.VMEM((total, HD), F32),
            pltpu.VMEM((total, wide), BF),
            pltpu.VMEM((total, wide), BF),
            pltpu.VMEM((SPANS, KV_HEADS, GROUP * rows, past + total), BF),
            pltpu.VMEM((total, pair), F32),
            pltpu.VMEM((total, wide), BF),
            pltpu.VMEM((total, pair), BF),
            pltpu.VMEM((rows, wide), BF),
        ]
        + [pltpu.VMEM((total, wide // XS), BF)] * XS,
    )
    state, back, empty, pieces = spare[:5], spare[5:8], spare[8], spare[9:]

    arrived = [empty] * LAG
    for step in range(steps):
        block_out, state = forward_call(step, rows, info, arrived[step], stream, weight, cached, state)
        arrived.append(hop(block_out, step, 1))
    kv, inv, normed, hidden, probs = state
    pieces, done = pieces_call(False, info, normed, pieces, back[2])
    back = (*back[:2], done)

    arrived = [empty] * LAG
    for step in range(steps):
        block_grad, back = backward_call(
            step, rows, sections, info, arrived[step], upstream, weight, cached, (kv, inv, normed, probs), back
        )
        arrived.append(hop(block_grad, step, -1))
        if step == SPANS:
            pieces, done = pieces_call(True, info, normed, pieces, back[2])
            back = (*back[:2], done)
    _, grad_in, done = back
    *pieces, done = lax.optimization_barrier((*pieces, done))
    share = summed_share(info, pieces, done)
    return (hidden[None, None], grad_in[None, None], share[None])


def solution(mesh):
    devices = mesh.devices.reshape(-1, YS, XS, CORES)
    dp = ("y", "x", "core")
    return jax.shard_map(
        body,
        mesh=Mesh(devices, ("section",) + dp),
        in_specs=(
            P(dp, None, None),
            P("section", None, None),
            P("section", dp, None, None),
            P(dp),
            P(dp, None, None),
        ),
        out_specs=(
            P("section", dp, None, None),
            P("section", dp, None, None),
            P("section", dp, None),
        ),
        check_vma=False,
    )
```

```python
import functools

import jax
import jax.numpy as jnp
from jax import lax
from jax.experimental import pallas as pl
from jax.experimental.pallas import tpu as pltpu
from jax.sharding import Mesh, PartitionSpec as P

HEADS = 32
KV_HEADS = 4
GROUP = HEADS // KV_HEADS
HD = 128
EPS = 1e-06
SCALE = HD ** (-0.5)
BF = jnp.bfloat16
F32 = jnp.float32
ANY = pl.BlockSpec(memory_space=pl.ANY)
VMEM = pl.BlockSpec(memory_space=pltpu.VMEM)
SMEM = pl.BlockSpec(memory_space=pltpu.SMEM)
TILE = 512
WIDTH = 1024
SPANS = 4
LAG = 2
WINDOW = 4
LIMIT = pltpu.CompilerParams(vmem_limit_bytes=24 * 2**20)


def dot_last(a, b):
    return lax.dot_general(a, b, (((1,), (1,)), ((), ())), preferred_element_type=F32)


def dot_first(a, b):
    return lax.dot_general(a, b, (((0,), (0,)), ((), ())), preferred_element_type=F32)


def in_hbm(a):
    return pltpu.with_memory_space_constraint(a, pltpu.HBM)


def in_vmem(a):
    return pltpu.with_memory_space_constraint(a, pltpu.VMEM)


def stack_heads(ref, group, rows):
    return jnp.concatenate(
        [ref[:, pl.ds((group * GROUP + h) * HD, HD)] for h in range(GROUP)], axis=0
    )


def load_kernel(count, info, *refs):
    sources, targets, sems = refs[:count], refs[count : 2 * count], refs[-1]
    copies = [pltpu.make_async_copy(sources[i], targets[i], sems.at[i]) for i in range(count)]
    for copy in copies:
        copy.start()
    for copy in copies:
        copy.wait()


def load_call(info, arrays, spare):
    count = len(arrays)
    out = [pltpu.VMEM(a.shape, a.dtype) for a in arrays] + list(spare)
    return pl.pallas_call(
        functools.partial(load_kernel, count),
        out_shape=tuple(out),
        in_specs=[SMEM] + [ANY] * count,
        out_specs=(ANY,) * len(out),
        scratch_shapes=[pltpu.SemaphoreType.DMA((count,))],
        compiler_params=LIMIT,
        name="load_weight",
    )(info, *[in_hbm(a) for a in arrays])


def forward_kernel(
    step, rows, fresh, info, incoming, tokens, weight, cached, kv_in, inv_in, normed_in, saved_in, probs_in,
    out, kv, inv_all, normed_all, saved, probs, x_buf, normed,
):
    turn = step - LAG * info[0]

    @pl.when(jnp.logical_and(turn >= 0, turn < SPANS))
    def _():
        block = jnp.clip(turn, 0, SPANS - 1)
        at = pl.multiple_of(block * rows, rows)
        mine = pl.ds(at, rows)
        block_in = incoming[...]
        if fresh:
            block_in = jnp.where(info[0] == 0, tokens[mine, :], block_in)
        x_buf[...] = block_in
        x = block_in.astype(F32)
        inv = lax.rsqrt(jnp.mean(x * x, axis=-1, keepdims=True) + EPS)
        inv_all[mine, :] = jnp.broadcast_to(inv, (rows, HD))
        low = (x * inv).astype(BF)
        normed[...] = low
        normed_all[mine, :] = low

        @pl.when(block == 0)
        def _():
            kv[...] = jnp.zeros_like(kv)

        @pl.loop(0, weight.shape[1] // TILE)
        def _(j):
            cols = pl.ds(pl.multiple_of(j * TILE, TILE), TILE)
            kv[mine, cols] = jnp.dot(
                normed[...], weight[:, cols], preferred_element_type=F32
            ).astype(BF)

        past = cached.shape[0]
        total = past + kv.shape[0]
        half = KV_HEADS * HD
        q_at = at + lax.broadcasted_iota(jnp.int32, (rows, total), 0)
        k_at = lax.broadcasted_iota(jnp.int32, (rows, total), 1)
        allowed = jnp.logical_or(
            k_at < info[1], jnp.logical_and(k_at >= past, k_at - past <= q_at)
        )
        bias = jnp.where(allowed, 0.0, -1e30)
        bias = jnp.concatenate([bias] * GROUP, axis=0)
        for g in range(KV_HEADS):
            k_cols = pl.ds(g * HD, HD)
            v_cols = pl.ds(half + g * HD, HD)
            keys = jnp.concatenate([cached[:, k_cols], kv[:, k_cols]], axis=0)
            values = jnp.concatenate([cached[:, v_cols], kv[:, v_cols]], axis=0)
            query = stack_heads(normed, g, rows)
            scores = dot_last(query, keys) * SCALE + bias
            top = jnp.max(scores, axis=-1, keepdims=True)
            e = jnp.exp(scores - top)
            p = (e * (1.0 / jnp.sum(e, axis=-1, keepdims=True))).astype(BF)
            probs[block, g] = p
            mixed = jnp.dot(p, values, preferred_element_type=F32)
            for h in range(GROUP):
                cols = pl.ds((g * GROUP + h) * HD, HD)
                sum_out = (
                    x_buf[:, cols].astype(F32) + mixed[h * rows : (h + 1) * rows]
                ).astype(BF)
                out[:, cols] = sum_out
                saved[mine, cols] = sum_out


def vmem_like(a):
    return pltpu.VMEM(a.shape, a.dtype)


def forward_call(step, rows, info, incoming, tokens, weight, cached, state):
    fresh = step < SPANS
    wide = weight.shape[0]
    tokens = tokens if fresh else incoming
    operands = [incoming, tokens, weight, cached, *state]
    res = pl.pallas_call(
        functools.partial(forward_kernel, step, rows, fresh),
        out_shape=(pltpu.VMEM((rows, wide), BF), *[vmem_like(a) for a in state]),
        in_specs=[SMEM] + [VMEM] * len(operands),
        out_specs=(VMEM,) * (1 + len(state)),
        scratch_shapes=[pltpu.VMEM((rows, wide), BF), pltpu.VMEM((rows, wide), BF)],
        input_output_aliases={5 + i: 1 + i for i in range(len(state))},
        compiler_params=LIMIT,
        name="forward_block",
    )(info, *[in_vmem(a) for a in operands])
    return res[0], res[1:]


def backward_kernel(
    step, rows, sections, fresh, info, incoming, cotangent, weight, cached, kv, inv_all, normed_all, probs,
    acc_in, grad_in0, done0, out, acc, grad_in, done, up_buf, gn,
):
    turn = step - LAG * (sections - 1 - info[0])

    @pl.when(jnp.logical_and(turn >= 0, turn < SPANS))
    def _():
        block = jnp.clip(SPANS - 1 - turn, 0, SPANS - 1)
        at = pl.multiple_of(block * rows, rows)
        mine = pl.ds(at, rows)
        block_up = incoming[...]
        if fresh:
            block_up = jnp.where(info[0] == sections - 1, cotangent[mine, :], block_up)
        up_buf[...] = block_up
        first = turn == 0
        past = cached.shape[0]
        half = KV_HEADS * HD
        for g in range(KV_HEADS):
            k_cols = pl.ds(g * HD, HD)
            v_cols = pl.ds(half + g * HD, HD)
            keys = jnp.concatenate([cached[:, k_cols], kv[:, k_cols]], axis=0)
            values = jnp.concatenate([cached[:, v_cols], kv[:, v_cols]], axis=0)
            query = jnp.concatenate(
                [normed_all[mine, pl.ds((g * GROUP + h) * HD, HD)] for h in range(GROUP)], axis=0
            )
            upstream = stack_heads(up_buf, g, rows)
            gp = dot_last(upstream, values)
            p_low = probs[block, g]
            p = p_low.astype(F32)
            inner = jnp.sum(p * gp, axis=-1, keepdims=True)
            ds = (p * (gp - inner) * SCALE).astype(BF)
            gq = jnp.dot(ds, keys, preferred_element_type=F32)
            for h in range(GROUP):
                gn[:, pl.ds((g * GROUP + h) * HD, HD)] = gq[h * rows : (h + 1) * rows]
            acc[:, k_cols] = jnp.where(first, 0.0, acc_in[:, k_cols]) + dot_first(
                ds[:, past:], query
            )
            acc[:, v_cols] = jnp.where(first, 0.0, acc_in[:, v_cols]) + dot_first(
                p_low[:, past:], upstream
            )
        grad_rows = acc[mine, :].astype(BF)
        done[mine, :] = grad_rows
        width = WIDTH

        def project(j, inner):
            cols = pl.ds(pl.multiple_of(j * width, width), width)
            part = gn[:, cols] + dot_last(grad_rows, weight[cols, :])
            gn[:, cols] = part
            term = part * normed_all[mine, cols].astype(F32)
            for i in range(width // HD):
                inner += term[:, i * HD : (i + 1) * HD]
            return inner

        inner = lax.fori_loop(0, weight.shape[0] // width, project, jnp.zeros((rows, HD), F32))
        inner = jnp.sum(inner, axis=-1, keepdims=True) * (1.0 / weight.shape[0])
        inv = inv_all[mine, :][:, :1]
        grad = (
            up_buf[...].astype(F32) + inv * (gn[...] - normed_all[mine, :].astype(F32) * inner)
        ).astype(BF)
        out[...] = grad
        grad_in[mine, :] = grad


def backward_call(step, rows, sections, info, incoming, cotangent, weight, cached, kept, state):
    fresh = step < SPANS
    wide = weight.shape[0]
    cotangent = cotangent if fresh else incoming
    operands = [incoming, cotangent, weight, cached, *kept, *state]
    start = 1 + len(operands) - len(state)
    res = pl.pallas_call(
        functools.partial(backward_kernel, step, rows, sections, fresh),
        out_shape=(pltpu.VMEM((rows, wide), BF), *[vmem_like(a) for a in state]),
        in_specs=[SMEM] + [VMEM] * len(operands),
        out_specs=(VMEM,) * (1 + len(state)),
        scratch_shapes=[pltpu.VMEM((rows, wide), BF), pltpu.VMEM((rows, wide), F32)],
        input_output_aliases={start + i: 1 + i for i in range(len(state))},
        compiler_params=LIMIT,
        name="backward_block",
    )(info, *[in_vmem(a) for a in operands])
    return res[0], res[1:]


YS, XS, CORES = 4, 4, 2


def pieces_kernel(late, info, normed, *refs):
    pieces = refs[1 + XS : 1 + 2 * XS]
    width = normed.shape[1] // (YS * XS)

    @pl.when((info[0] == info[2]) == late)
    def _():
        for k, piece in enumerate(pieces):
            x = lax.rem(info[4] + k, XS)
            for y in range(YS):
                cols = pl.ds(pl.multiple_of((y * XS + x) * width, width), width)
                piece[:, y * width : (y + 1) * width] = normed[:, cols]


def pieces_call(late, info, normed, pieces, done):
    *pieces, done = pl.pallas_call(
        functools.partial(pieces_kernel, late),
        out_shape=tuple(vmem_like(a) for a in (*pieces, done)),
        in_specs=[SMEM] + [VMEM] * (2 + XS),
        out_specs=(VMEM,) * (1 + XS),
        input_output_aliases={2 + i: i for i in range(1 + XS)},
        compiler_params=LIMIT,
        name="column_pieces",
    )(info, in_vmem(normed), *[in_vmem(a) for a in pieces], in_vmem(done))
    return pieces, done


def product_kernel(info, *refs):
    columns, grads = refs[:XS], refs[XS : 2 * XS]
    away, mine, left, right = refs[2 * XS :]
    rows, width = columns[0].shape[0], columns[0].shape[1] // (YS * CORES)
    for d in range(XS):
        left[pl.ds(d * rows, rows), :] = columns[d][...]
        right[pl.ds(d * rows, rows), :] = grads[d][...]

    @pl.loop(0, YS)
    def _(j):
        y = lax.rem(info[3] + j, YS)
        for core in range(CORES):
            whose = jnp.where(core == 0, 1 - info[5], info[5])
            cols = pl.ds(pl.multiple_of((y * CORES + whose) * width, width), width)
            part = dot_first(left[:, cols], right[...])
            if core == 0:
                away[j] = part.astype(BF)
            else:
                mine[j] = part


def product_call(info, columns, grads):
    rows, pair = grads[0].shape
    width = columns[0].shape[1] // (YS * CORES)
    return pl.pallas_call(
        product_kernel,
        out_shape=(pltpu.VMEM((YS, width, pair), BF), pltpu.VMEM((YS, width, pair), F32)),
        in_specs=[SMEM] + [VMEM] * (2 * XS),
        out_specs=(VMEM, VMEM),
        scratch_shapes=[
            pltpu.VMEM((XS * rows, columns[0].shape[1]), BF),
            pltpu.VMEM((XS * rows, pair), BF),
        ],
        compiler_params=LIMIT,
        name="document_product",
    )(info, *[in_vmem(a) for a in columns], *[in_vmem(a) for a in grads])


def merge_kernel(mine, other, *parts):
    parts[0][...] = mine[0] + other[0].astype(F32)
    for j in range(1, YS):
        parts[j][...] = (mine[j] + other[j].astype(F32)).astype(BF)


def merge_call(mine, other):
    shape = mine.shape[1:]
    return pl.pallas_call(
        merge_kernel,
        out_shape=tuple(pltpu.VMEM(shape, F32 if j == 0 else BF) for j in range(YS)),
        in_specs=[VMEM, VMEM],
        out_specs=(VMEM,) * YS,
        compiler_params=LIMIT,
        name="merge_cores",
    )(in_vmem(mine), in_vmem(other))


def from_offset(value, axis, by):
    size = lax.axis_size(axis)
    return lax.ppermute(value, axis, [((i + by) % size, i) for i in range(size)])


def summed_share(info, pieces, grad_rows):
    grads = [grad_rows] + [from_offset(grad_rows, "x", d) for d in range(1, XS)]
    columns = [pieces[0]] + [from_offset(pieces[XS - d], "x", d) for d in range(1, XS)]
    away, mine = product_call(info, columns, grads)
    total, *parts = merge_call(mine, from_offset(away, "core", 1))
    for j, part in enumerate(parts, 1):
        total = total + from_offset(part, "y", -j).astype(F32)
    return total


def body(tokens, kv_weight, cache_kv, cached_len, cotangent):
    at = lax.axis_index("section")
    sections = lax.axis_size("section")
    total, wide = tokens.shape[1:]
    pair = kv_weight.shape[2]
    rows = total // SPANS
    past = cache_kv.shape[2]
    steps = LAG * (sections - 1) + SPANS
    where = [lax.axis_index(axis) for axis in ("y", "x", "core")]
    info = jnp.stack([at, cached_len[0], sections - 1, *where]).astype(jnp.int32)

    def hop(value, step, by):
        window = range(step - step % WINDOW, step - step % WINDOW + WINDOW)
        movers = [
            (s, s + by)
            for s in range(sections)
            if 0 <= s + by < sections
            and any(0 <= t - LAG * (s if by > 0 else sections - 1 - s) < SPANS for t in window)
        ]
        needed = step < LAG * (sections - 2) + SPANS
        return lax.ppermute(value, "section", movers) if needed else None

    weight, cached, stream, upstream, *spare = load_call(
        info,
        [kv_weight[0], cache_kv[0, 0], tokens[0], cotangent[0]],
        [
            pltpu.VMEM((total, pair), BF),
            pltpu.VMEM((total, HD), F32),
            pltpu.VMEM((total, wide), BF),
            pltpu.VMEM((total, wide), BF),
            pltpu.VMEM((SPANS, KV_HEADS, GROUP * rows, past + total), BF),
            pltpu.VMEM((total, pair), F32),
            pltpu.VMEM((total, wide), BF),
            pltpu.VMEM((total, pair), BF),
            pltpu.VMEM((rows, wide), BF),
        ]
        + [pltpu.VMEM((total, wide // XS), BF)] * XS,
    )
    state, back, empty, pieces = spare[:5], spare[5:8], spare[8], spare[9:]

    arrived = [empty] * LAG
    for step in range(steps):
        block_out, state = forward_call(step, rows, info, arrived[step], stream, weight, cached, state)
        arrived.append(hop(block_out, step, 1))
    kv, inv, normed, hidden, probs = state
    pieces, done = pieces_call(False, info, normed, pieces, back[2])
    back = (*back[:2], done)

    arrived = [empty] * LAG
    for step in range(steps):
        block_grad, back = backward_call(
            step, rows, sections, info, arrived[step], upstream, weight, cached, (kv, inv, normed, probs), back
        )
        arrived.append(hop(block_grad, step, -1))
        if step == SPANS:
            pieces, done = pieces_call(True, info, normed, pieces, back[2])
            back = (*back[:2], done)
    _, grad_in, done = back
    *pieces, done = lax.optimization_barrier((*pieces, done))
    share = summed_share(info, pieces, done)
    return (hidden[None, None], grad_in[None, None], share[None])


def solution(mesh):
    devices = mesh.devices.reshape(-1, YS, XS, CORES)
    dp = ("y", "x", "core")
    return jax.shard_map(
        body,
        mesh=Mesh(devices, ("section",) + dp),
        in_specs=(
            P(dp, None, None),
            P("section", None, None),
            P("section", dp, None, None),
            P(dp),
            P(dp, None, None),
        ),
        out_specs=(
            P("section", dp, None, None),
            P("section", dp, None, None),
            P("section", dp, None),
        ),
        check_vma=False,
    )
```

```python
import functools

import jax
import jax.numpy as jnp
from jax import lax
from jax.experimental import pallas as pl
from jax.experimental.pallas import tpu as pltpu
from jax.sharding import Mesh, PartitionSpec as P

HEADS = 32
KV_HEADS = 4
GROUP = HEADS // KV_HEADS
HD = 128
EPS = 1e-06
SCALE = HD ** (-0.5)
BF = jnp.bfloat16
F32 = jnp.float32
ANY = pl.BlockSpec(memory_space=pl.ANY)
VMEM = pl.BlockSpec(memory_space=pltpu.VMEM)
SMEM = pl.BlockSpec(memory_space=pltpu.SMEM)
TILE = 512
WIDTH = 1024
SPANS = 4
LAG = 2
WINDOW = 4
EARLY = 4
LIMIT = pltpu.CompilerParams(vmem_limit_bytes=24 * 2**20)


def dot_last(a, b):
    return lax.dot_general(a, b, (((1,), (1,)), ((), ())), preferred_element_type=F32)


def dot_first(a, b):
    return lax.dot_general(a, b, (((0,), (0,)), ((), ())), preferred_element_type=F32)


def in_hbm(a):
    return pltpu.with_memory_space_constraint(a, pltpu.HBM)


def in_vmem(a):
    return pltpu.with_memory_space_constraint(a, pltpu.VMEM)


def stack_heads(ref, group, rows):
    return jnp.concatenate(
        [ref[:, pl.ds((group * GROUP + h) * HD, HD)] for h in range(GROUP)], axis=0
    )


def load_kernel(count, info, *refs):
    sources, targets, sems = refs[:count], refs[count : 2 * count], refs[-1]
    copies = [pltpu.make_async_copy(sources[i], targets[i], sems.at[i]) for i in range(count)]
    for copy in copies:
        copy.start()
    for copy in copies:
        copy.wait()


def load_call(info, arrays, spare):
    count = len(arrays)
    out = [pltpu.VMEM(a.shape, a.dtype) for a in arrays] + list(spare)
    return pl.pallas_call(
        functools.partial(load_kernel, count),
        out_shape=tuple(out),
        in_specs=[SMEM] + [ANY] * count,
        out_specs=(ANY,) * len(out),
        scratch_shapes=[pltpu.SemaphoreType.DMA((count,))],
        compiler_params=LIMIT,
        name="load_weight",
    )(info, *[in_hbm(a) for a in arrays])


def forward_kernel(
    step, rows, fresh, info, incoming, tokens, weight, cached, kv_in, inv_in, normed_in, saved_in, probs_in,
    turned_in, out, kv, inv_all, normed_all, saved, probs, turned, x_buf, normed,
):
    turn = step - LAG * info[0]

    @pl.when(jnp.logical_and(turn >= 0, turn < SPANS))
    def _():
        block = jnp.clip(turn, 0, SPANS - 1)
        at = pl.multiple_of(block * rows, rows)
        mine = pl.ds(at, rows)
        block_in = incoming[...]
        if fresh:
            block_in = jnp.where(info[0] == 0, tokens[mine, :], block_in)
        x_buf[...] = block_in
        x = block_in.astype(F32)
        inv = lax.rsqrt(jnp.mean(x * x, axis=-1, keepdims=True) + EPS)
        inv_all[mine, :] = jnp.broadcast_to(inv, (rows, HD))
        low = (x * inv).astype(BF)
        normed[...] = low
        normed_all[mine, :] = low

        @pl.when(block == 0)
        def _():
            kv[...] = jnp.zeros_like(kv)

        @pl.loop(0, weight.shape[1] // TILE)
        def _(j):
            cols = pl.ds(pl.multiple_of(j * TILE, TILE), TILE)
            kv[mine, cols] = jnp.dot(
                normed[...], weight[:, cols], preferred_element_type=F32
            ).astype(BF)

        past = cached.shape[0]
        total = past + kv.shape[0]
        half = KV_HEADS * HD
        q_at = at + lax.broadcasted_iota(jnp.int32, (rows, total), 0)
        k_at = lax.broadcasted_iota(jnp.int32, (rows, total), 1)
        allowed = jnp.logical_or(
            k_at < info[1], jnp.logical_and(k_at >= past, k_at - past <= q_at)
        )
        bias = jnp.where(allowed, 0.0, -1e30)
        bias = jnp.concatenate([bias] * GROUP, axis=0)
        for g in range(KV_HEADS):
            k_cols = pl.ds(g * HD, HD)
            v_cols = pl.ds(half + g * HD, HD)
            keys = jnp.concatenate([cached[:, k_cols], kv[:, k_cols]], axis=0)
            values = jnp.concatenate([cached[:, v_cols], kv[:, v_cols]], axis=0)
            query = stack_heads(normed, g, rows)
            scores = dot_last(query, keys) * SCALE + bias
            top = jnp.max(scores, axis=-1, keepdims=True)
            e = jnp.exp(scores - top)
            p = (e * (1.0 / jnp.sum(e, axis=-1, keepdims=True))).astype(BF)
            probs[block, g] = p
            mixed = jnp.dot(p, values, preferred_element_type=F32)
            for h in range(GROUP):
                cols = pl.ds((g * GROUP + h) * HD, HD)
                sum_out = (
                    x_buf[:, cols].astype(F32) + mixed[h * rows : (h + 1) * rows]
                ).astype(BF)
                out[:, cols] = sum_out
                saved[mine, cols] = sum_out


def vmem_like(a):
    return pltpu.VMEM(a.shape, a.dtype)


def forward_call(step, rows, info, incoming, tokens, weight, cached, state):
    fresh = step < SPANS
    wide = weight.shape[0]
    tokens = tokens if fresh else incoming
    operands = [incoming, tokens, weight, cached, *state]
    res = pl.pallas_call(
        functools.partial(forward_kernel, step, rows, fresh),
        out_shape=(pltpu.VMEM((rows, wide), BF), *[vmem_like(a) for a in state]),
        in_specs=[SMEM] + [VMEM] * len(operands),
        out_specs=(VMEM,) * (1 + len(state)),
        scratch_shapes=[pltpu.VMEM((rows, wide), BF), pltpu.VMEM((rows, wide), BF)],
        input_output_aliases={5 + i: 1 + i for i in range(len(state))},
        compiler_params=LIMIT,
        name="forward_block",
    )(info, *[in_vmem(a) for a in operands])
    return res[0], res[1:]


def backward_kernel(
    step, rows, sections, fresh, info, incoming, cotangent, weight, cached, kv, inv_all, normed_all, probs,
    acc_in, grad_in0, done0, out, acc, grad_in, done, up_buf, gn,
):
    turn = step - LAG * (sections - 1 - info[0])

    @pl.when(jnp.logical_and(turn >= 0, turn < SPANS))
    def _():
        block = jnp.clip(SPANS - 1 - turn, 0, SPANS - 1)
        at = pl.multiple_of(block * rows, rows)
        mine = pl.ds(at, rows)
        block_up = incoming[...]
        if fresh:
            block_up = jnp.where(info[0] == sections - 1, cotangent[mine, :], block_up)
        up_buf[...] = block_up
        first = turn == 0
        past = cached.shape[0]
        half = KV_HEADS * HD
        for g in range(KV_HEADS):
            k_cols = pl.ds(g * HD, HD)
            v_cols = pl.ds(half + g * HD, HD)
            keys = jnp.concatenate([cached[:, k_cols], kv[:, k_cols]], axis=0)
            values = jnp.concatenate([cached[:, v_cols], kv[:, v_cols]], axis=0)
            query = jnp.concatenate(
                [normed_all[mine, pl.ds((g * GROUP + h) * HD, HD)] for h in range(GROUP)], axis=0
            )
            upstream = stack_heads(up_buf, g, rows)
            gp = dot_last(upstream, values)
            p_low = probs[block, g]
            p = p_low.astype(F32)
            inner = jnp.sum(p * gp, axis=-1, keepdims=True)
            ds = (p * (gp - inner) * SCALE).astype(BF)
            gq = jnp.dot(ds, keys, preferred_element_type=F32)
            for h in range(GROUP):
                gn[:, pl.ds((g * GROUP + h) * HD, HD)] = gq[h * rows : (h + 1) * rows]
            acc[:, k_cols] = jnp.where(first, 0.0, acc_in[:, k_cols]) + dot_first(
                ds[:, past:], query
            )
            acc[:, v_cols] = jnp.where(first, 0.0, acc_in[:, v_cols]) + dot_first(
                p_low[:, past:], upstream
            )
        grad_rows = acc[mine, :].astype(BF)
        done[mine, :] = grad_rows
        width = WIDTH

        def project(j, inner):
            cols = pl.ds(pl.multiple_of(j * width, width), width)
            part = gn[:, cols] + jnp.dot(grad_rows, weight[:, cols], preferred_element_type=F32)
            gn[:, cols] = part
            term = part * normed_all[mine, cols].astype(F32)
            for i in range(width // HD):
                inner += term[:, i * HD : (i + 1) * HD]
            return inner

        inner = lax.fori_loop(0, weight.shape[1] // width, project, jnp.zeros((rows, HD), F32))
        inner = jnp.sum(inner, axis=-1, keepdims=True) * (1.0 / weight.shape[1])
        inv = inv_all[mine, :][:, :1]
        grad = (
            up_buf[...].astype(F32) + inv * (gn[...] - normed_all[mine, :].astype(F32) * inner)
        ).astype(BF)
        out[...] = grad
        grad_in[mine, :] = grad


def backward_call(step, rows, sections, info, incoming, cotangent, weight, cached, kept, state):
    fresh = step < SPANS
    wide = weight.shape[1]
    cotangent = cotangent if fresh else incoming
    operands = [incoming, cotangent, weight, cached, *kept, *state]
    start = 1 + len(operands) - len(state)
    res = pl.pallas_call(
        functools.partial(backward_kernel, step, rows, sections, fresh),
        out_shape=(pltpu.VMEM((rows, wide), BF), *[vmem_like(a) for a in state]),
        in_specs=[SMEM] + [VMEM] * len(operands),
        out_specs=(VMEM,) * (1 + len(state)),
        scratch_shapes=[pltpu.VMEM((rows, wide), BF), pltpu.VMEM((rows, wide), F32)],
        input_output_aliases={start + i: 1 + i for i in range(len(state))},
        compiler_params=LIMIT,
        name="backward_block",
    )(info, *[in_vmem(a) for a in operands])
    return res[0], res[1:]


YS, XS, CORES = 4, 4, 2


def flip_kernel(late, info, weight, passed_in, turned_in, passed, turned):
    step = 256

    @pl.when((info[0] == 0) == late)
    def _():
        @pl.loop(0, weight.shape[0] // step)
        def _(i):
            part = pl.ds(pl.multiple_of(i * step, step), step)
            turned[:, part] = weight[part, :].T


def flip_call(late, info, weight, passed, turned):
    return pl.pallas_call(
        functools.partial(flip_kernel, late),
        out_shape=(vmem_like(passed), vmem_like(turned)),
        in_specs=[SMEM] + [VMEM] * 3,
        out_specs=(VMEM, VMEM),
        input_output_aliases={2: 0, 3: 1},
        compiler_params=LIMIT,
        name="flip_weight",
    )(info, in_vmem(weight), in_vmem(passed), in_vmem(turned))


def pieces_kernel(late, info, normed, *refs):
    pieces = refs[1 + XS : 1 + 2 * XS]
    width = normed.shape[1] // (YS * XS)

    @pl.when((info[0] >= EARLY) == late)
    def _():
        for k, piece in enumerate(pieces):
            x = lax.rem(info[4] + k, XS)
            for y in range(YS):
                cols = pl.ds(pl.multiple_of((y * XS + x) * width, width), width)
                piece[:, y * width : (y + 1) * width] = normed[:, cols]


def pieces_call(late, info, normed, pieces, passed):
    *pieces, passed = pl.pallas_call(
        functools.partial(pieces_kernel, late),
        out_shape=tuple(vmem_like(a) for a in (*pieces, passed)),
        in_specs=[SMEM] + [VMEM] * (2 + XS),
        out_specs=(VMEM,) * (1 + XS),
        input_output_aliases={2 + i: i for i in range(1 + XS)},
        compiler_params=LIMIT,
        name="column_pieces",
    )(info, in_vmem(normed), *[in_vmem(a) for a in pieces], in_vmem(passed))
    return pieces, passed


def settle_call(arrays):
    return pl.pallas_call(
        lambda *refs: None,
        out_shape=tuple(vmem_like(a) for a in arrays),
        in_specs=[VMEM] * len(arrays),
        out_specs=(VMEM,) * len(arrays),
        input_output_aliases={i: i for i in range(len(arrays))},
        compiler_params=LIMIT,
        name="settle",
    )(*[in_vmem(a) for a in arrays])


def product_kernel(info, *refs):
    early, columns, grads = refs[: XS - 1], refs[XS - 1 : 2 * XS - 1], refs[2 * XS - 1 : 3 * XS - 1]
    away, mine, left, right = refs[3 * XS - 1 :]
    rows, width = columns[0].shape[0], columns[0].shape[1] // (YS * CORES)
    for d in range(XS):
        part = columns[d][...]
        if d > 0:
            part = jnp.where(info[0] < EARLY, early[d - 1][...], part)
        left[pl.ds(d * rows, rows), :] = part
        right[pl.ds(d * rows, rows), :] = grads[d][...]

    @pl.loop(0, YS)
    def _(j):
        y = lax.rem(info[3] + j, YS)
        for core in range(CORES):
            whose = jnp.where(core == 0, 1 - info[5], info[5])
            cols = pl.ds(pl.multiple_of((y * CORES + whose) * width, width), width)
            part = dot_first(left[:, cols], right[...])
            if core == 0:
                away[j] = part.astype(BF)
            else:
                mine[j] = part


def product_call(info, early, columns, grads):
    rows, pair = grads[0].shape
    width = columns[0].shape[1] // (YS * CORES)
    return pl.pallas_call(
        product_kernel,
        out_shape=(pltpu.VMEM((YS, width, pair), BF), pltpu.VMEM((YS, width, pair), F32)),
        in_specs=[SMEM] + [VMEM] * (3 * XS - 1),
        out_specs=(VMEM, VMEM),
        scratch_shapes=[
            pltpu.VMEM((XS * rows, columns[0].shape[1]), BF),
            pltpu.VMEM((XS * rows, pair), BF),
        ],
        compiler_params=LIMIT,
        name="document_product",
    )(info, *[in_vmem(a) for a in (*early, *columns, *grads)])


def merge_kernel(mine, other, *parts):
    parts[0][...] = mine[0] + other[0].astype(F32)
    for j in range(1, YS):
        parts[j][...] = (mine[j] + other[j].astype(F32)).astype(BF)


def merge_call(mine, other):
    shape = mine.shape[1:]
    return pl.pallas_call(
        merge_kernel,
        out_shape=tuple(pltpu.VMEM(shape, F32 if j == 0 else BF) for j in range(YS)),
        in_specs=[VMEM, VMEM],
        out_specs=(VMEM,) * YS,
        compiler_params=LIMIT,
        name="merge_cores",
    )(in_vmem(mine), in_vmem(other))


def from_offset(value, axis, by):
    size = lax.axis_size(axis)
    return lax.ppermute(value, axis, [((i + by) % size, i) for i in range(size)])


def columns_from(pieces, members):
    found = []
    for d in range(1, XS):
        pairs = [(s * XS + (i + d) % XS, s * XS + i) for s in members for i in range(XS)]
        found.append(lax.ppermute(pieces[XS - d], ("section", "x"), pairs))
    return found


def summed_share(info, early, columns, grad_rows):
    grads = [grad_rows] + [from_offset(grad_rows, "x", d) for d in range(1, XS)]
    away, mine = product_call(info, early, columns, grads)
    total, *parts = merge_call(mine, from_offset(away, "core", 1))
    for j, part in enumerate(parts, 1):
        total = total + from_offset(part, "y", -j).astype(F32)
    return total


def body(tokens, kv_weight, cache_kv, cached_len, cotangent):
    at = lax.axis_index("section")
    sections = lax.axis_size("section")
    total, wide = tokens.shape[1:]
    pair = kv_weight.shape[2]
    rows = total // SPANS
    past = cache_kv.shape[2]
    steps = LAG * (sections - 1) + SPANS
    where = [lax.axis_index(axis) for axis in ("y", "x", "core")]
    info = jnp.stack([at, cached_len[0], sections - 1, *where]).astype(jnp.int32)

    def hop(value, step, by):
        window = range(step - step % WINDOW, step - step % WINDOW + WINDOW)
        movers = [
            (s, s + by)
            for s in range(sections)
            if 0 <= s + by < sections
            and any(0 <= t - LAG * (s if by > 0 else sections - 1 - s) < SPANS for t in window)
        ]
        needed = step < LAG * (sections - 2) + SPANS
        return lax.ppermute(value, "section", movers) if needed else None

    weight, cached, stream, upstream, *spare = load_call(
        info,
        [kv_weight[0], cache_kv[0, 0], tokens[0], cotangent[0]],
        [
            pltpu.VMEM((total, pair), BF),
            pltpu.VMEM((total, HD), F32),
            pltpu.VMEM((total, wide), BF),
            pltpu.VMEM((total, wide), BF),
            pltpu.VMEM((SPANS, KV_HEADS, GROUP * rows, past + total), BF),
            pltpu.VMEM((total, pair), F32),
            pltpu.VMEM((total, wide), BF),
            pltpu.VMEM((total, pair), BF),
            pltpu.VMEM((rows, wide), BF),
        ]
        + [pltpu.VMEM((total, wide // XS), BF)] * XS
        + [pltpu.VMEM((pair, wide), BF)],
    )
    state, back, empty, pieces, turned = spare[:5], spare[5:8], spare[8], spare[9:-1], spare[-1]
    state[1], turned = flip_call(False, info, weight, state[1], turned)
    state = [*state, turned]

    arrived = [empty] * LAG
    for step in range(steps):
        block_out, state = forward_call(step, rows, info, arrived[step], stream, weight, cached, state)
        arrived.append(hop(block_out, step, 1))
        state = list(state)
        if step == SPANS:
            state[1], state[5] = flip_call(True, info, weight, state[1], state[5])
        if step == steps - SPANS - LAG:
            pieces, state[3] = pieces_call(False, info, state[2], pieces, state[3])
        if step == steps - SPANS - 1:
            early = columns_from(pieces, range(EARLY))
    kv, inv, normed, hidden, probs, turned = state
    arrived = [empty] * LAG
    for step in range(steps):
        block_grad, back = backward_call(
            step, rows, sections, info, arrived[step], upstream, turned, cached, (kv, inv, normed, probs), back
        )
        arrived.append(hop(block_grad, step, -1))
        if step == SPANS:
            *early, done = settle_call((*early, back[2]))
            back = (*back[:2], done)
        if step == LAG * (sections - 1 - EARLY) + SPANS:
            pieces, done = pieces_call(True, info, normed, pieces, back[2])
            back = (*back[:2], done)
    _, grad_in, done = back
    *pieces, done = lax.optimization_barrier((*pieces, done))
    columns = [pieces[0]] + columns_from(pieces, range(EARLY, sections))
    share = summed_share(info, early, columns, done)
    return (hidden[None, None], grad_in[None, None], share[None])


def solution(mesh):
    devices = mesh.devices.reshape(-1, YS, XS, CORES)
    dp = ("y", "x", "core")
    return jax.shard_map(
        body,
        mesh=Mesh(devices, ("section",) + dp),
        in_specs=(
            P(dp, None, None),
            P("section", None, None),
            P("section", dp, None, None),
            P(dp),
            P(dp, None, None),
        ),
        out_specs=(
            P("section", dp, None, None),
            P("section", dp, None, None),
            P("section", dp, None),
        ),
        check_vma=False,
    )
```

```python
import functools

import jax
import jax.numpy as jnp
from jax import lax
from jax.experimental import pallas as pl
from jax.experimental.pallas import tpu as pltpu
from jax.sharding import Mesh, PartitionSpec as P

HEADS = 32
KV_HEADS = 4
GROUP = HEADS // KV_HEADS
HD = 128
EPS = 1e-06
SCALE = HD ** (-0.5)
BF = jnp.bfloat16
F32 = jnp.float32
ANY = pl.BlockSpec(memory_space=pl.ANY)
VMEM = pl.BlockSpec(memory_space=pltpu.VMEM)
SMEM = pl.BlockSpec(memory_space=pltpu.SMEM)
TILE = 512
WIDTH = 1024
SPANS = 4
LAG = 2
WINDOW = 4
EARLY = 4
LIMIT = pltpu.CompilerParams(vmem_limit_bytes=12 * 2**20)


def dot_last(a, b):
    return lax.dot_general(a, b, (((1,), (1,)), ((), ())), preferred_element_type=F32)


def dot_first(a, b):
    return lax.dot_general(a, b, (((0,), (0,)), ((), ())), preferred_element_type=F32)


def in_hbm(a):
    return pltpu.with_memory_space_constraint(a, pltpu.HBM)


def in_vmem(a):
    return pltpu.with_memory_space_constraint(a, pltpu.VMEM)


def stack_heads(ref, group, rows):
    return jnp.concatenate(
        [ref[:, pl.ds((group * GROUP + h) * HD, HD)] for h in range(GROUP)], axis=0
    )


def load_kernel(count, info, *refs):
    sources, targets, sems = refs[:count], refs[count : 2 * count], refs[-1]
    copies = [pltpu.make_async_copy(sources[i], targets[i], sems.at[i]) for i in range(count)]
    for copy in copies:
        copy.start()
    for copy in copies:
        copy.wait()


def load_call(info, arrays, spare):
    count = len(arrays)
    out = [pltpu.VMEM(a.shape, a.dtype) for a in arrays] + list(spare)
    return pl.pallas_call(
        functools.partial(load_kernel, count),
        out_shape=tuple(out),
        in_specs=[SMEM] + [ANY] * count,
        out_specs=(ANY,) * len(out),
        scratch_shapes=[pltpu.SemaphoreType.DMA((count,))],
        compiler_params=LIMIT,
        name="load_weight",
    )(info, *[in_hbm(a) for a in arrays])


def forward_kernel(
    step, rows, fresh, info, incoming, tokens, weight, cached, kv_in, inv_in, normed_in, saved_in, probs_in,
    turned_in, out, kv, inv_all, normed_all, saved, probs, turned, x_buf, normed,
):
    turn = step - LAG * info[0]

    @pl.when(jnp.logical_and(turn >= 0, turn < SPANS))
    def _():
        block = jnp.clip(turn, 0, SPANS - 1)
        at = pl.multiple_of(block * rows, rows)
        mine = pl.ds(at, rows)
        block_in = incoming[...]
        if fresh:
            block_in = jnp.where(info[0] == 0, tokens[mine, :], block_in)
        x_buf[...] = block_in
        x = block_in.astype(F32)
        inv = lax.rsqrt(jnp.mean(x * x, axis=-1, keepdims=True) + EPS)
        inv_all[mine, :] = jnp.broadcast_to(inv, (rows, HD))
        low = (x * inv).astype(BF)
        normed[...] = low
        normed_all[mine, :] = low

        @pl.when(block == 0)
        def _():
            kv[...] = jnp.zeros_like(kv)

        @pl.loop(0, weight.shape[1] // TILE)
        def _(j):
            cols = pl.ds(pl.multiple_of(j * TILE, TILE), TILE)
            kv[mine, cols] = jnp.dot(
                normed[...], weight[:, cols], preferred_element_type=F32
            ).astype(BF)

        past = cached.shape[0]
        total = past + kv.shape[0]
        half = KV_HEADS * HD
        q_at = at + lax.broadcasted_iota(jnp.int32, (rows, total), 0)
        k_at = lax.broadcasted_iota(jnp.int32, (rows, total), 1)
        allowed = jnp.logical_or(
            k_at < info[1], jnp.logical_and(k_at >= past, k_at - past <= q_at)
        )
        bias = jnp.where(allowed, 0.0, -1e30)
        bias = jnp.concatenate([bias] * GROUP, axis=0)
        for g in range(KV_HEADS):
            k_cols = pl.ds(g * HD, HD)
            v_cols = pl.ds(half + g * HD, HD)
            keys = jnp.concatenate([cached[:, k_cols], kv[:, k_cols]], axis=0)
            values = jnp.concatenate([cached[:, v_cols], kv[:, v_cols]], axis=0)
            query = stack_heads(normed, g, rows)
            scores = dot_last(query, keys) * SCALE + bias
            top = jnp.max(scores, axis=-1, keepdims=True)
            e = jnp.exp(scores - top)
            p = (e * (1.0 / jnp.sum(e, axis=-1, keepdims=True))).astype(BF)
            probs[block, g] = p
            mixed = jnp.dot(p, values, preferred_element_type=F32)
            for h in range(GROUP):
                cols = pl.ds((g * GROUP + h) * HD, HD)
                sum_out = (
                    x_buf[:, cols].astype(F32) + mixed[h * rows : (h + 1) * rows]
                ).astype(BF)
                out[:, cols] = sum_out
                saved[mine, cols] = sum_out


def vmem_like(a):
    return pltpu.VMEM(a.shape, a.dtype)


def forward_call(step, rows, info, incoming, tokens, weight, cached, state):
    fresh = step < SPANS
    wide = weight.shape[0]
    tokens = tokens if fresh else incoming
    operands = [incoming, tokens, weight, cached, *state]
    res = pl.pallas_call(
        functools.partial(forward_kernel, step, rows, fresh),
        out_shape=(pltpu.VMEM((rows, wide), BF), *[vmem_like(a) for a in state]),
        in_specs=[SMEM] + [VMEM] * len(operands),
        out_specs=(VMEM,) * (1 + len(state)),
        scratch_shapes=[pltpu.VMEM((rows, wide), BF), pltpu.VMEM((rows, wide), BF)],
        input_output_aliases={5 + i: 1 + i for i in range(len(state))},
        compiler_params=LIMIT,
        name="forward_block",
    )(info, *[in_vmem(a) for a in operands])
    return res[0], res[1:]


def backward_kernel(
    step, rows, sections, fresh, info, incoming, cotangent, weight, cached, kv, inv_all, normed_all, probs,
    acc_in, grad_in0, done0, out, acc, grad_in, done, up_buf, gn,
):
    turn = step - LAG * (sections - 1 - info[0])

    @pl.when(jnp.logical_and(turn >= 0, turn < SPANS))
    def _():
        block = jnp.clip(SPANS - 1 - turn, 0, SPANS - 1)
        at = pl.multiple_of(block * rows, rows)
        mine = pl.ds(at, rows)
        block_up = incoming[...]
        if fresh:
            block_up = jnp.where(info[0] == sections - 1, cotangent[mine, :], block_up)
        up_buf[...] = block_up
        first = turn == 0
        past = cached.shape[0]
        half = KV_HEADS * HD
        inner = jnp.zeros((rows, HD), F32)
        for g in range(KV_HEADS):
            k_cols = pl.ds(g * HD, HD)
            v_cols = pl.ds(half + g * HD, HD)
            keys = jnp.concatenate([cached[:, k_cols], kv[:, k_cols]], axis=0)
            values = jnp.concatenate([cached[:, v_cols], kv[:, v_cols]], axis=0)
            query = jnp.concatenate(
                [normed_all[mine, pl.ds((g * GROUP + h) * HD, HD)] for h in range(GROUP)], axis=0
            )
            upstream = stack_heads(up_buf, g, rows)
            gp = dot_last(upstream, values)
            p_low = probs[block, g]
            p = p_low.astype(F32)
            mean = jnp.sum(p * gp, axis=-1, keepdims=True)
            ds = (p * (gp - mean) * SCALE).astype(BF)
            gq = jnp.dot(ds, keys, preferred_element_type=F32)
            terms = gq * query.astype(F32)
            for h in range(GROUP):
                gn[:, pl.ds((g * GROUP + h) * HD, HD)] = gq[h * rows : (h + 1) * rows]
                inner += terms[h * rows : (h + 1) * rows]
            acc[:, k_cols] = jnp.where(first, 0.0, acc_in[:, k_cols]) + dot_first(
                ds[:, past:], query
            )
            acc[:, v_cols] = jnp.where(first, 0.0, acc_in[:, v_cols]) + dot_first(
                p_low[:, past:], upstream
            )
        grad_rows = acc[mine, :].astype(BF)
        done[mine, :] = grad_rows
        terms = grad_rows.astype(F32) * kv[mine, :].astype(F32)
        for i in range(grad_rows.shape[1] // HD):
            inner += terms[:, i * HD : (i + 1) * HD]
        wide = weight.shape[1]
        inner = jnp.sum(inner, axis=-1, keepdims=True) * (1.0 / wide)
        inv = inv_all[mine, :][:, :1]
        width = WIDTH

        for j in range(wide // width):
            cols = pl.ds(j * width, width)
            part = gn[:, cols] + jnp.dot(grad_rows, weight[:, cols], preferred_element_type=F32)
            grad = (
                up_buf[:, cols].astype(F32)
                + inv * (part - normed_all[mine, cols].astype(F32) * inner)
            ).astype(BF)
            out[:, cols] = grad
            grad_in[mine, cols] = grad


def backward_call(step, rows, sections, info, incoming, cotangent, weight, cached, kept, state):
    fresh = step < SPANS
    wide = weight.shape[1]
    cotangent = cotangent if fresh else incoming
    operands = [incoming, cotangent, weight, cached, *kept, *state]
    start = 1 + len(operands) - len(state)
    res = pl.pallas_call(
        functools.partial(backward_kernel, step, rows, sections, fresh),
        out_shape=(pltpu.VMEM((rows, wide), BF), *[vmem_like(a) for a in state]),
        in_specs=[SMEM] + [VMEM] * len(operands),
        out_specs=(VMEM,) * (1 + len(state)),
        scratch_shapes=[pltpu.VMEM((rows, wide), BF), pltpu.VMEM((rows, wide), F32)],
        input_output_aliases={start + i: 1 + i for i in range(len(state))},
        compiler_params=LIMIT,
        name="backward_block",
    )(info, *[in_vmem(a) for a in operands])
    return res[0], res[1:]


YS, XS, CORES = 4, 4, 2


def flip_kernel(late, info, weight, passed_in, turned_in, passed, turned):
    step = 256

    @pl.when((info[0] == 0) == late)
    def _():
        @pl.loop(0, weight.shape[0] // step)
        def _(i):
            part = pl.ds(pl.multiple_of(i * step, step), step)
            turned[:, part] = weight[part, :].T


def flip_call(late, info, weight, passed, turned):
    return pl.pallas_call(
        functools.partial(flip_kernel, late),
        out_shape=(vmem_like(passed), vmem_like(turned)),
        in_specs=[SMEM] + [VMEM] * 3,
        out_specs=(VMEM, VMEM),
        input_output_aliases={2: 0, 3: 1},
        compiler_params=LIMIT,
        name="flip_weight",
    )(info, in_vmem(weight), in_vmem(passed), in_vmem(turned))


def pieces_kernel(late, info, normed, *refs):
    pieces = refs[1 + XS : 1 + 2 * XS]
    width = normed.shape[1] // (YS * XS)

    @pl.when((info[0] >= EARLY) == late)
    def _():
        for k, piece in enumerate(pieces):
            x = lax.rem(info[4] + k, XS)
            for y in range(YS):
                cols = pl.ds(pl.multiple_of((y * XS + x) * width, width), width)
                piece[:, y * width : (y + 1) * width] = normed[:, cols]


def pieces_call(late, info, normed, pieces, passed):
    *pieces, passed = pl.pallas_call(
        functools.partial(pieces_kernel, late),
        out_shape=tuple(vmem_like(a) for a in (*pieces, passed)),
        in_specs=[SMEM] + [VMEM] * (2 + XS),
        out_specs=(VMEM,) * (1 + XS),
        input_output_aliases={2 + i: i for i in range(1 + XS)},
        compiler_params=LIMIT,
        name="column_pieces",
    )(info, in_vmem(normed), *[in_vmem(a) for a in pieces], in_vmem(passed))
    return pieces, passed


def settle_call(arrays):
    return pl.pallas_call(
        lambda *refs: None,
        out_shape=tuple(vmem_like(a) for a in arrays),
        in_specs=[VMEM] * len(arrays),
        out_specs=(VMEM,) * len(arrays),
        input_output_aliases={i: i for i in range(len(arrays))},
        compiler_params=LIMIT,
        name="settle",
    )(*[in_vmem(a) for a in arrays])


def product_kernel(info, *refs):
    early, columns, grads = refs[: XS - 1], refs[XS - 1 : 2 * XS - 1], refs[2 * XS - 1 : 3 * XS - 1]
    away, mine, left, right = refs[3 * XS - 1 :]
    rows, width = columns[0].shape[0], columns[0].shape[1] // (YS * CORES)
    for d in range(XS):
        part = columns[d][...]
        if d > 0:
            part = jnp.where(info[0] < EARLY, early[d - 1][...], part)
        left[pl.ds(d * rows, rows), :] = part
        right[pl.ds(d * rows, rows), :] = grads[d][...]

    @pl.loop(0, YS)
    def _(j):
        y = lax.rem(info[3] + j, YS)
        for core in range(CORES):
            whose = jnp.where(core == 0, 1 - info[5], info[5])
            cols = pl.ds(pl.multiple_of((y * CORES + whose) * width, width), width)
            part = dot_first(left[:, cols], right[...])
            if core == 0:
                away[j] = part.astype(BF)
            else:
                mine[j] = part


def product_call(info, early, columns, grads):
    rows, pair = grads[0].shape
    width = columns[0].shape[1] // (YS * CORES)
    return pl.pallas_call(
        product_kernel,
        out_shape=(pltpu.VMEM((YS, width, pair), BF), pltpu.VMEM((YS, width, pair), F32)),
        in_specs=[SMEM] + [VMEM] * (3 * XS - 1),
        out_specs=(VMEM, VMEM),
        scratch_shapes=[
            pltpu.VMEM((XS * rows, columns[0].shape[1]), BF),
            pltpu.VMEM((XS * rows, pair), BF),
        ],
        compiler_params=LIMIT,
        name="document_product",
    )(info, *[in_vmem(a) for a in (*early, *columns, *grads)])


def merge_kernel(mine, other, *parts):
    parts[0][...] = mine[0] + other[0].astype(F32)
    for j in range(1, YS):
        parts[j][...] = (mine[j] + other[j].astype(F32)).astype(BF)


def merge_call(mine, other):
    shape = mine.shape[1:]
    return pl.pallas_call(
        merge_kernel,
        out_shape=tuple(pltpu.VMEM(shape, F32 if j == 0 else BF) for j in range(YS)),
        in_specs=[VMEM, VMEM],
        out_specs=(VMEM,) * YS,
        compiler_params=LIMIT,
        name="merge_cores",
    )(in_vmem(mine), in_vmem(other))


def from_offset(value, axis, by):
    size = lax.axis_size(axis)
    return lax.ppermute(value, axis, [((i + by) % size, i) for i in range(size)])


def columns_from(pieces, members):
    found = []
    for d in range(1, XS):
        pairs = [(s * XS + (i + d) % XS, s * XS + i) for s in members for i in range(XS)]
        found.append(lax.ppermute(pieces[XS - d], ("section", "x"), pairs))
    return found


def summed_share(info, early, columns, grad_rows):
    grads = [grad_rows] + [from_offset(grad_rows, "x", d) for d in range(1, XS)]
    away, mine = product_call(info, early, columns, grads)
    total, *parts = merge_call(mine, from_offset(away, "core", 1))
    for j, part in enumerate(parts, 1):
        total = total + from_offset(part, "y", -j).astype(F32)
    return total


def body(tokens, kv_weight, cache_kv, cached_len, cotangent):
    at = lax.axis_index("section")
    sections = lax.axis_size("section")
    total, wide = tokens.shape[1:]
    pair = kv_weight.shape[2]
    rows = total // SPANS
    past = cache_kv.shape[2]
    steps = LAG * (sections - 1) + SPANS
    where = [lax.axis_index(axis) for axis in ("y", "x", "core")]
    info = jnp.stack([at, cached_len[0], sections - 1, *where]).astype(jnp.int32)

    def hop(value, step, by):
        window = range(step - step % WINDOW, step - step % WINDOW + WINDOW)
        movers = [
            (s, s + by)
            for s in range(sections)
            if 0 <= s + by < sections
            and any(0 <= t - LAG * (s if by > 0 else sections - 1 - s) < SPANS for t in window)
        ]
        needed = step < LAG * (sections - 2) + SPANS
        return lax.ppermute(value, "section", movers) if needed else None

    weight, cached, stream, upstream, *spare = load_call(
        info,
        [kv_weight[0], cache_kv[0, 0], tokens[0], cotangent[0]],
        [
            pltpu.VMEM((total, pair), BF),
            pltpu.VMEM((total, HD), F32),
            pltpu.VMEM((total, wide), BF),
            pltpu.VMEM((total, wide), BF),
            pltpu.VMEM((SPANS, KV_HEADS, GROUP * rows, past + total), BF),
            pltpu.VMEM((total, pair), F32),
            pltpu.VMEM((total, wide), BF),
            pltpu.VMEM((total, pair), BF),
            pltpu.VMEM((rows, wide), BF),
        ]
        + [pltpu.VMEM((total, wide // XS), BF)] * XS
        + [pltpu.VMEM((pair, wide), BF)],
    )
    state, back, empty, pieces, turned = spare[:5], spare[5:8], spare[8], spare[9:-1], spare[-1]
    state[1], turned = flip_call(False, info, weight, state[1], turned)
    state = [*state, turned]

    arrived = [empty] * LAG
    for step in range(steps):
        block_out, state = forward_call(step, rows, info, arrived[step], stream, weight, cached, state)
        arrived.append(hop(block_out, step, 1))
        state = list(state)
        if step == SPANS:
            state[1], state[5] = flip_call(True, info, weight, state[1], state[5])
        if step == steps - SPANS - LAG:
            pieces, state[3] = pieces_call(False, info, state[2], pieces, state[3])
        if step == steps - SPANS - 1:
            early = columns_from(pieces, range(EARLY))
    kv, inv, normed, hidden, probs, turned = state
    arrived = [empty] * LAG
    for step in range(steps):
        block_grad, back = backward_call(
            step, rows, sections, info, arrived[step], upstream, turned, cached, (kv, inv, normed, probs), back
        )
        arrived.append(hop(block_grad, step, -1))
        if step == SPANS:
            *early, done = settle_call((*early, back[2]))
            back = (*back[:2], done)
        if step == LAG * (sections - 1 - EARLY) + SPANS:
            pieces, done = pieces_call(True, info, normed, pieces, back[2])
            back = (*back[:2], done)
    _, grad_in, done = back
    *pieces, done = lax.optimization_barrier((*pieces, done))
    columns = [pieces[0]] + columns_from(pieces, range(EARLY, sections))
    share = summed_share(info, early, columns, done)
    return (hidden[None, None], grad_in[None, None], share[None])


def solution(mesh):
    devices = mesh.devices.reshape(-1, YS, XS, CORES)
    dp = ("y", "x", "core")
    return jax.shard_map(
        body,
        mesh=Mesh(devices, ("section",) + dp),
        in_specs=(
            P(dp, None, None),
            P("section", None, None),
            P("section", dp, None, None),
            P(dp),
            P(dp, None, None),
        ),
        out_specs=(
            P("section", dp, None, None),
            P("section", dp, None, None),
            P("section", dp, None),
        ),
        check_vma=False,
    )
```

```python
import functools

import jax
import jax.numpy as jnp
from jax import lax
from jax.experimental import pallas as pl
from jax.experimental.pallas import tpu as pltpu
from jax.sharding import Mesh, PartitionSpec as P

HEADS = 32
KV_HEADS = 4
GROUP = HEADS // KV_HEADS
HD = 128
EPS = 1e-06
SCALE = HD ** (-0.5)
BF = jnp.bfloat16
F32 = jnp.float32
ANY = pl.BlockSpec(memory_space=pl.ANY)
VMEM = pl.BlockSpec(memory_space=pltpu.VMEM)
SMEM = pl.BlockSpec(memory_space=pltpu.SMEM)
TILE = 512
WIDTH = 1024
SPANS = 4
LAG = 2
WINDOW = 4
EARLY = 4
LIMIT = pltpu.CompilerParams(vmem_limit_bytes=12 * 2**20)


def dot_last(a, b):
    return lax.dot_general(a, b, (((1,), (1,)), ((), ())), preferred_element_type=F32)


def dot_first(a, b):
    return lax.dot_general(a, b, (((0,), (0,)), ((), ())), preferred_element_type=F32)


def in_hbm(a):
    return pltpu.with_memory_space_constraint(a, pltpu.HBM)


def in_vmem(a):
    return pltpu.with_memory_space_constraint(a, pltpu.VMEM)


def stack_heads(ref, group, rows):
    return jnp.concatenate(
        [ref[:, pl.ds((group * GROUP + h) * HD, HD)] for h in range(GROUP)], axis=0
    )


def flip(weight, turned):
    step = 256

    @pl.loop(0, weight.shape[0] // step)
    def _(i):
        part = pl.ds(pl.multiple_of(i * step, step), step)
        turned[:, part] = weight[part, :].T


def cut_pieces(info, normed, pieces):
    width = normed.shape[1] // (YS * XS)
    for k, piece in enumerate(pieces):
        x = lax.rem(info[4] + k, XS)
        for y in range(YS):
            cols = pl.ds(pl.multiple_of((y * XS + x) * width, width), width)
            piece[:, y * width : (y + 1) * width] = normed[:, cols]


def load_kernel(count, info, *refs):
    sources, targets, sems = refs[:count], refs[count : 2 * count], refs[-1]
    copies = [pltpu.make_async_copy(sources[i], targets[i], sems.at[i]) for i in range(count)]
    for copy in copies:
        copy.start()
    for copy in copies:
        copy.wait()


def load_call(info, arrays, spare):
    count = len(arrays)
    out = [pltpu.VMEM(a.shape, a.dtype) for a in arrays] + list(spare)
    return pl.pallas_call(
        functools.partial(load_kernel, count),
        out_shape=tuple(out),
        in_specs=[SMEM] + [ANY] * count,
        out_specs=(ANY,) * len(out),
        scratch_shapes=[pltpu.SemaphoreType.DMA((count,))],
        compiler_params=LIMIT,
        name="load_weight",
    )(info, *[in_hbm(a) for a in arrays])


def forward_kernel(step, rows, fresh, count, info, incoming, tokens, weight, cached, *refs):
    out, kv, inv_all, normed_all, saved, probs, turned, *pieces, x_buf, normed = refs[count:]
    if step in (0, SPANS):

        @pl.when((info[0] == 0) == (step > 0))
        def _():
            flip(weight, turned)

    if pieces:

        @pl.when(info[0] < EARLY)
        def _():
            cut_pieces(info, normed_all, pieces)

    turn = step - LAG * info[0]

    @pl.when(jnp.logical_and(turn >= 0, turn < SPANS))
    def _():
        block = jnp.clip(turn, 0, SPANS - 1)
        at = pl.multiple_of(block * rows, rows)
        mine = pl.ds(at, rows)
        block_in = incoming[...]
        if fresh:
            block_in = jnp.where(info[0] == 0, tokens[mine, :], block_in)
        x_buf[...] = block_in
        x = block_in.astype(F32)
        inv = lax.rsqrt(jnp.mean(x * x, axis=-1, keepdims=True) + EPS)
        inv_all[mine, :] = jnp.broadcast_to(inv, (rows, HD))
        low = (x * inv).astype(BF)
        normed[...] = low
        normed_all[mine, :] = low

        @pl.when(block == 0)
        def _():
            kv[...] = jnp.zeros_like(kv)

        @pl.loop(0, weight.shape[1] // TILE)
        def _(j):
            cols = pl.ds(pl.multiple_of(j * TILE, TILE), TILE)
            kv[mine, cols] = jnp.dot(
                normed[...], weight[:, cols], preferred_element_type=F32
            ).astype(BF)

        past = cached.shape[0]
        total = past + kv.shape[0]
        half = KV_HEADS * HD
        q_at = at + lax.broadcasted_iota(jnp.int32, (rows, total), 0)
        k_at = lax.broadcasted_iota(jnp.int32, (rows, total), 1)
        allowed = jnp.logical_or(
            k_at < info[1], jnp.logical_and(k_at >= past, k_at - past <= q_at)
        )
        bias = jnp.where(allowed, 0.0, -1e30)
        bias = jnp.concatenate([bias] * GROUP, axis=0)
        for g in range(KV_HEADS):
            k_cols = pl.ds(g * HD, HD)
            v_cols = pl.ds(half + g * HD, HD)
            keys = jnp.concatenate([cached[:, k_cols], kv[:, k_cols]], axis=0)
            values = jnp.concatenate([cached[:, v_cols], kv[:, v_cols]], axis=0)
            query = stack_heads(normed, g, rows)
            scores = dot_last(query, keys) * SCALE + bias
            top = jnp.max(scores, axis=-1, keepdims=True)
            e = jnp.exp(scores - top)
            p = (e * (1.0 / jnp.sum(e, axis=-1, keepdims=True))).astype(BF)
            probs[block, g] = p
            mixed = jnp.dot(p, values, preferred_element_type=F32)
            for h in range(GROUP):
                cols = pl.ds((g * GROUP + h) * HD, HD)
                sum_out = (
                    x_buf[:, cols].astype(F32) + mixed[h * rows : (h + 1) * rows]
                ).astype(BF)
                out[:, cols] = sum_out
                saved[mine, cols] = sum_out


def vmem_like(a):
    return pltpu.VMEM(a.shape, a.dtype)


def forward_call(step, rows, info, incoming, tokens, weight, cached, state):
    fresh = step < SPANS
    wide = weight.shape[0]
    tokens = tokens if fresh else incoming
    operands = [incoming, tokens, weight, cached, *state]
    res = pl.pallas_call(
        functools.partial(forward_kernel, step, rows, fresh, len(state)),
        out_shape=(pltpu.VMEM((rows, wide), BF), *[vmem_like(a) for a in state]),
        in_specs=[SMEM] + [VMEM] * len(operands),
        out_specs=(VMEM,) * (1 + len(state)),
        scratch_shapes=[pltpu.VMEM((rows, wide), BF), pltpu.VMEM((rows, wide), BF)],
        input_output_aliases={5 + i: 1 + i for i in range(len(state))},
        compiler_params=LIMIT,
        name="forward_block",
    )(info, *[in_vmem(a) for a in operands])
    return res[0], res[1:]


def backward_kernel(
    step, rows, sections, fresh, count, extra, info, incoming, cotangent, weight, cached, kv, inv_all,
    normed_all, probs, *refs,
):
    acc_in = refs[extra]
    out, acc, grad_in, done, *pieces, up_buf, gn = refs[extra + count :]
    if pieces:

        @pl.when(info[0] >= EARLY)
        def _():
            cut_pieces(info, normed_all, pieces)

    turn = step - LAG * (sections - 1 - info[0])

    @pl.when(jnp.logical_and(turn >= 0, turn < SPANS))
    def _():
        block = jnp.clip(SPANS - 1 - turn, 0, SPANS - 1)
        at = pl.multiple_of(block * rows, rows)
        mine = pl.ds(at, rows)
        block_up = incoming[...]
        if fresh:
            block_up = jnp.where(info[0] == sections - 1, cotangent[mine, :], block_up)
        up_buf[...] = block_up
        first = turn == 0
        past = cached.shape[0]
        half = KV_HEADS * HD
        inner = jnp.zeros((rows, HD), F32)
        for g in range(KV_HEADS):
            k_cols = pl.ds(g * HD, HD)
            v_cols = pl.ds(half + g * HD, HD)
            keys = jnp.concatenate([cached[:, k_cols], kv[:, k_cols]], axis=0)
            values = jnp.concatenate([cached[:, v_cols], kv[:, v_cols]], axis=0)
            query = jnp.concatenate(
                [normed_all[mine, pl.ds((g * GROUP + h) * HD, HD)] for h in range(GROUP)], axis=0
            )
            upstream = stack_heads(up_buf, g, rows)
            gp = dot_last(upstream, values)
            p_low = probs[block, g]
            p = p_low.astype(F32)
            mean = jnp.sum(p * gp, axis=-1, keepdims=True)
            ds = (p * (gp - mean) * SCALE).astype(BF)
            gq = jnp.dot(ds, keys, preferred_element_type=F32)
            terms = gq * query.astype(F32)
            for h in range(GROUP):
                gn[:, pl.ds((g * GROUP + h) * HD, HD)] = gq[h * rows : (h + 1) * rows]
                inner += terms[h * rows : (h + 1) * rows]
            acc[:, k_cols] = jnp.where(first, 0.0, acc_in[:, k_cols]) + dot_first(
                ds[:, past:], query
            )
            acc[:, v_cols] = jnp.where(first, 0.0, acc_in[:, v_cols]) + dot_first(
                p_low[:, past:], upstream
            )
        grad_rows = acc[mine, :].astype(BF)
        done[mine, :] = grad_rows
        terms = grad_rows.astype(F32) * kv[mine, :].astype(F32)
        for i in range(grad_rows.shape[1] // HD):
            inner += terms[:, i * HD : (i + 1) * HD]
        wide = weight.shape[1]
        inner = jnp.sum(inner, axis=-1, keepdims=True) * (1.0 / wide)
        inv = inv_all[mine, :][:, :1]
        width = WIDTH

        for j in range(wide // width):
            cols = pl.ds(j * width, width)
            part = gn[:, cols] + jnp.dot(grad_rows, weight[:, cols], preferred_element_type=F32)
            grad = (
                up_buf[:, cols].astype(F32)
                + inv * (part - normed_all[mine, cols].astype(F32) * inner)
            ).astype(BF)
            out[:, cols] = grad
            grad_in[mine, cols] = grad


def backward_call(step, rows, sections, info, incoming, cotangent, weight, cached, kept, extra, state):
    fresh = step < SPANS
    wide = weight.shape[1]
    cotangent = cotangent if fresh else incoming
    operands = [incoming, cotangent, weight, cached, *kept, *extra, *state]
    start = 1 + len(operands) - len(state)
    res = pl.pallas_call(
        functools.partial(backward_kernel, step, rows, sections, fresh, len(state), len(extra)),
        out_shape=(pltpu.VMEM((rows, wide), BF), *[vmem_like(a) for a in state]),
        in_specs=[SMEM] + [VMEM] * len(operands),
        out_specs=(VMEM,) * (1 + len(state)),
        scratch_shapes=[pltpu.VMEM((rows, wide), BF), pltpu.VMEM((rows, wide), F32)],
        input_output_aliases={start + i: 1 + i for i in range(len(state))},
        compiler_params=LIMIT,
        name="backward_block",
    )(info, *[in_vmem(a) for a in operands])
    return res[0], res[1:]


YS, XS, CORES = 4, 4, 2


def product_kernel(info, *refs):
    early, columns, grads = refs[: XS - 1], refs[XS - 1 : 2 * XS - 1], refs[2 * XS - 1 : 3 * XS - 1]
    away, mine, left, right = refs[3 * XS - 1 :]
    rows, width = columns[0].shape[0], columns[0].shape[1] // (YS * CORES)
    for d in range(XS):
        part = columns[d][...]
        if d > 0:
            part = jnp.where(info[0] < EARLY, early[d - 1][...], part)
        left[pl.ds(d * rows, rows), :] = part
        right[pl.ds(d * rows, rows), :] = grads[d][...]

    @pl.loop(0, YS)
    def _(j):
        y = lax.rem(info[3] + j, YS)
        for core in range(CORES):
            whose = jnp.where(core == 0, 1 - info[5], info[5])
            cols = pl.ds(pl.multiple_of((y * CORES + whose) * width, width), width)
            part = dot_first(left[:, cols], right[...])
            if core == 0:
                away[j] = part.astype(BF)
            else:
                mine[j] = part


def product_call(info, early, columns, grads):
    rows, pair = grads[0].shape
    width = columns[0].shape[1] // (YS * CORES)
    return pl.pallas_call(
        product_kernel,
        out_shape=(pltpu.VMEM((YS, width, pair), BF), pltpu.VMEM((YS, width, pair), F32)),
        in_specs=[SMEM] + [VMEM] * (3 * XS - 1),
        out_specs=(VMEM, VMEM),
        scratch_shapes=[
            pltpu.VMEM((XS * rows, columns[0].shape[1]), BF),
            pltpu.VMEM((XS * rows, pair), BF),
        ],
        compiler_params=LIMIT,
        name="document_product",
    )(info, *[in_vmem(a) for a in (*early, *columns, *grads)])


def merge_kernel(mine, other, *parts):
    parts[0][...] = mine[0] + other[0].astype(F32)
    for j in range(1, YS):
        parts[j][...] = (mine[j] + other[j].astype(F32)).astype(BF)


def merge_call(mine, other):
    shape = mine.shape[1:]
    return pl.pallas_call(
        merge_kernel,
        out_shape=tuple(pltpu.VMEM(shape, F32 if j == 0 else BF) for j in range(YS)),
        in_specs=[VMEM, VMEM],
        out_specs=(VMEM,) * YS,
        compiler_params=LIMIT,
        name="merge_cores",
    )(in_vmem(mine), in_vmem(other))


def from_offset(value, axis, by):
    size = lax.axis_size(axis)
    return lax.ppermute(value, axis, [((i + by) % size, i) for i in range(size)])


def columns_from(pieces, members):
    found = []
    for d in range(1, XS):
        pairs = [(s * XS + (i + d) % XS, s * XS + i) for s in members for i in range(XS)]
        found.append(lax.ppermute(pieces[XS - d], ("section", "x"), pairs))
    return found


def summed_share(info, early, columns, grad_rows):
    grads = [grad_rows] + [from_offset(grad_rows, "x", d) for d in range(1, XS)]
    away, mine = product_call(info, early, columns, grads)
    total, *parts = merge_call(mine, from_offset(away, "core", 1))
    for j, part in enumerate(parts, 1):
        total = total + from_offset(part, "y", -j).astype(F32)
    return total


def body(tokens, kv_weight, cache_kv, cached_len, cotangent):
    at = lax.axis_index("section")
    sections = lax.axis_size("section")
    total, wide = tokens.shape[1:]
    pair = kv_weight.shape[2]
    rows = total // SPANS
    past = cache_kv.shape[2]
    steps = LAG * (sections - 1) + SPANS
    where = [lax.axis_index(axis) for axis in ("y", "x", "core")]
    info = jnp.stack([at, cached_len[0], sections - 1, *where]).astype(jnp.int32)

    def hop(value, step, by):
        window = range(step - step % WINDOW, step - step % WINDOW + WINDOW)
        movers = [
            (s, s + by)
            for s in range(sections)
            if 0 <= s + by < sections
            and any(0 <= t - LAG * (s if by > 0 else sections - 1 - s) < SPANS for t in window)
        ]
        needed = step < LAG * (sections - 2) + SPANS
        return lax.ppermute(value, "section", movers) if needed else None

    weight, cached, stream, upstream, *spare = load_call(
        info,
        [kv_weight[0], cache_kv[0, 0], tokens[0], cotangent[0]],
        [
            pltpu.VMEM((total, pair), BF),
            pltpu.VMEM((total, HD), F32),
            pltpu.VMEM((total, wide), BF),
            pltpu.VMEM((total, wide), BF),
            pltpu.VMEM((SPANS, KV_HEADS, GROUP * rows, past + total), BF),
            pltpu.VMEM((total, pair), F32),
            pltpu.VMEM((total, wide), BF),
            pltpu.VMEM((total, pair), BF),
            pltpu.VMEM((rows, wide), BF),
        ]
        + [pltpu.VMEM((total, wide // XS), BF)] * XS
        + [pltpu.VMEM((pair, wide), BF)],
    )
    state, back, empty, pieces, turned = spare[:5], spare[5:8], spare[8], spare[9:-1], spare[-1]
    state = [*state, turned]

    arrived = [empty] * LAG
    for step in range(steps):
        if step == steps - SPANS - LAG:
            state = [*state, *pieces]
        block_out, state = forward_call(step, rows, info, arrived[step], stream, weight, cached, state)
        arrived.append(hop(block_out, step, 1))
        state, pieces = state[:6], state[6:] or pieces
    kv, inv, normed, hidden, probs, turned = state
    early = columns_from(pieces, range(EARLY))
    wanted = {2 * i + 3: [piece] for i, piece in enumerate(early)}

    arrived = [empty] * LAG
    for step in range(steps):
        turn = step == LAG * (sections - 1 - EARLY) + SPANS
        if turn:
            back = [*back, *pieces]
        block_grad, back = backward_call(
            step, rows, sections, info, arrived[step], upstream, turned, cached, (kv, inv, normed, probs),
            wanted.get(step, []), back,
        )
        arrived.append(hop(block_grad, step, -1))
        if turn:
            back, pieces = back[:3], back[3:]
            late = columns_from(pieces, range(EARLY, sections))
            wanted = {step + 2 * i + 3: [piece] for i, piece in enumerate(late)}
    _, grad_in, done = back
    columns = [pieces[0], *late]
    share = summed_share(info, early, columns, done)
    return (hidden[None, None], grad_in[None, None], share[None])


def solution(mesh):
    devices = mesh.devices.reshape(-1, YS, XS, CORES)
    dp = ("y", "x", "core")
    return jax.shard_map(
        body,
        mesh=Mesh(devices, ("section",) + dp),
        in_specs=(
            P(dp, None, None),
            P("section", None, None),
            P("section", dp, None, None),
            P(dp),
            P(dp, None, None),
        ),
        out_specs=(
            P("section", dp, None, None),
            P("section", dp, None, None),
            P("section", dp, None),
        ),
        check_vma=False,
    )
```

```python
import functools

import jax
import jax.numpy as jnp
from jax import lax
from jax.experimental import pallas as pl
from jax.experimental.pallas import tpu as pltpu
from jax.sharding import Mesh, PartitionSpec as P

HEADS = 32
KV_HEADS = 4
GROUP = HEADS // KV_HEADS
HD = 128
EPS = 1e-06
SCALE = HD ** (-0.5)
BF = jnp.bfloat16
F32 = jnp.float32
ANY = pl.BlockSpec(memory_space=pl.ANY)
VMEM = pl.BlockSpec(memory_space=pltpu.VMEM)
SMEM = pl.BlockSpec(memory_space=pltpu.SMEM)
TILE = 512
WIDTH = 1024
SPANS = 4
LAG = 2
WINDOW = 4
EARLY = 4
LIMIT = pltpu.CompilerParams(vmem_limit_bytes=12 * 2**20)


def dot_last(a, b):
    return lax.dot_general(a, b, (((1,), (1,)), ((), ())), preferred_element_type=F32)


def dot_first(a, b):
    return lax.dot_general(a, b, (((0,), (0,)), ((), ())), preferred_element_type=F32)


def in_hbm(a):
    return pltpu.with_memory_space_constraint(a, pltpu.HBM)


def in_vmem(a):
    return pltpu.with_memory_space_constraint(a, pltpu.VMEM)


def stack_heads(ref, group, rows):
    return jnp.concatenate(
        [ref[:, pl.ds((group * GROUP + h) * HD, HD)] for h in range(GROUP)], axis=0
    )


def flip(weight, turned):
    step = 256

    @pl.loop(0, weight.shape[0] // step)
    def _(i):
        part = pl.ds(pl.multiple_of(i * step, step), step)
        turned[:, part] = weight[part, :].T


def cut_pieces(info, normed, pieces):
    width = normed.shape[1] // (YS * XS)
    for k, piece in enumerate(pieces):
        x = lax.rem(info[4] + k, XS)
        for y in range(YS):
            cols = pl.ds(pl.multiple_of((y * XS + x) * width, width), width)
            piece[:, y * width : (y + 1) * width] = normed[:, cols]


def load_kernel(count, info, *refs):
    sources, targets, sems = refs[:count], refs[count : 2 * count], refs[-1]
    copies = [pltpu.make_async_copy(sources[i], targets[i], sems.at[i]) for i in range(count)]
    for copy in copies:
        copy.start()
    for copy in copies:
        copy.wait()


def load_call(info, arrays, spare):
    count = len(arrays)
    out = [pltpu.VMEM(a.shape, a.dtype) for a in arrays] + list(spare)
    return pl.pallas_call(
        functools.partial(load_kernel, count),
        out_shape=tuple(out),
        in_specs=[SMEM] + [ANY] * count,
        out_specs=(ANY,) * len(out),
        scratch_shapes=[pltpu.SemaphoreType.DMA((count,))],
        compiler_params=LIMIT,
        name="load_weight",
    )(info, *[in_hbm(a) for a in arrays])


def forward_kernel(step, rows, fresh, count, info, incoming, tokens, weight, cached, *refs):
    out, kv, inv_all, normed_all, saved, probs, turned, *pieces, x_buf, normed = refs[count:]
    if step in (0, SPANS):

        @pl.when((info[0] == 0) == (step > 0))
        def _():
            flip(weight, turned)

    if pieces:

        @pl.when(info[0] < EARLY)
        def _():
            cut_pieces(info, normed_all, pieces)

    turn = step - LAG * info[0]

    @pl.when(jnp.logical_and(turn >= 0, turn < SPANS))
    def _():
        block = jnp.clip(turn, 0, SPANS - 1)
        at = pl.multiple_of(block * rows, rows)
        mine = pl.ds(at, rows)
        block_in = incoming[...]
        if fresh:
            block_in = jnp.where(info[0] == 0, tokens[mine, :], block_in)
        x_buf[...] = block_in
        x = block_in.astype(F32)
        inv = lax.rsqrt(jnp.mean(x * x, axis=-1, keepdims=True) + EPS)
        inv_all[mine, :] = jnp.broadcast_to(inv, (rows, HD))
        low = (x * inv).astype(BF)
        normed[...] = low
        normed_all[mine, :] = low

        @pl.when(block == 0)
        def _():
            kv[...] = jnp.zeros_like(kv)

        @pl.loop(0, weight.shape[1] // TILE)
        def _(j):
            cols = pl.ds(pl.multiple_of(j * TILE, TILE), TILE)
            kv[mine, cols] = jnp.dot(
                normed[...], weight[:, cols], preferred_element_type=F32
            ).astype(BF)

        past = cached.shape[0]
        total = past + kv.shape[0]
        half = KV_HEADS * HD
        q_at = at + lax.broadcasted_iota(jnp.int32, (rows, total), 0)
        k_at = lax.broadcasted_iota(jnp.int32, (rows, total), 1)
        allowed = jnp.logical_or(
            k_at < info[1], jnp.logical_and(k_at >= past, k_at - past <= q_at)
        )
        bias = jnp.where(allowed, 0.0, -1e30)
        bias = jnp.concatenate([bias] * GROUP, axis=0)
        for g in range(KV_HEADS):
            k_cols = pl.ds(g * HD, HD)
            v_cols = pl.ds(half + g * HD, HD)
            keys = jnp.concatenate([cached[:, k_cols], kv[:, k_cols]], axis=0)
            values = jnp.concatenate([cached[:, v_cols], kv[:, v_cols]], axis=0)
            query = stack_heads(normed, g, rows)
            scores = dot_last(query, keys) * SCALE + bias
            top = jnp.max(scores, axis=-1, keepdims=True)
            e = jnp.exp(scores - top)
            p = (e * (1.0 / jnp.sum(e, axis=-1, keepdims=True))).astype(BF)
            probs[block, g] = p
            mixed = jnp.dot(p, values, preferred_element_type=F32)
            for h in range(GROUP):
                cols = pl.ds((g * GROUP + h) * HD, HD)
                sum_out = (
                    x_buf[:, cols].astype(F32) + mixed[h * rows : (h + 1) * rows]
                ).astype(BF)
                out[:, cols] = sum_out
                saved[mine, cols] = sum_out


def vmem_like(a):
    return pltpu.VMEM(a.shape, a.dtype)


def forward_call(step, rows, info, incoming, tokens, weight, cached, state):
    fresh = step < SPANS
    wide = weight.shape[0]
    tokens = tokens if fresh else incoming
    operands = [incoming, tokens, weight, cached, *state]
    res = pl.pallas_call(
        functools.partial(forward_kernel, step, rows, fresh, len(state)),
        out_shape=(pltpu.VMEM((rows, wide), BF), *[vmem_like(a) for a in state]),
        in_specs=[SMEM] + [VMEM] * len(operands),
        out_specs=(VMEM,) * (1 + len(state)),
        scratch_shapes=[pltpu.VMEM((rows, wide), BF), pltpu.VMEM((rows, wide), BF)],
        input_output_aliases={5 + i: 1 + i for i in range(len(state))},
        compiler_params=LIMIT,
        name="forward_block",
    )(info, *[in_vmem(a) for a in operands])
    return res[0], res[1:]


def backward_kernel(
    step, rows, sections, fresh, count, extra, info, incoming, cotangent, weight, cached, kv, inv_all,
    normed_all, probs, *refs,
):
    acc_in = refs[extra]
    out, acc, grad_in, done, *pieces, up_buf, gn = refs[extra + count :]
    if pieces:

        @pl.when(info[0] >= EARLY)
        def _():
            cut_pieces(info, normed_all, pieces)

    turn = step - LAG * (sections - 1 - info[0])

    @pl.when(jnp.logical_and(turn >= 0, turn < SPANS))
    def _():
        block = jnp.clip(SPANS - 1 - turn, 0, SPANS - 1)
        at = pl.multiple_of(block * rows, rows)
        mine = pl.ds(at, rows)
        block_up = incoming[...]
        if fresh:
            block_up = jnp.where(info[0] == sections - 1, cotangent[mine, :], block_up)
        up_buf[...] = block_up
        first = turn == 0
        past = cached.shape[0]
        half = KV_HEADS * HD
        inner = jnp.zeros((rows, HD), F32)
        for g in range(KV_HEADS):
            k_cols = pl.ds(g * HD, HD)
            v_cols = pl.ds(half + g * HD, HD)
            keys = jnp.concatenate([cached[:, k_cols], kv[:, k_cols]], axis=0)
            values = jnp.concatenate([cached[:, v_cols], kv[:, v_cols]], axis=0)
            query = jnp.concatenate(
                [normed_all[mine, pl.ds((g * GROUP + h) * HD, HD)] for h in range(GROUP)], axis=0
            )
            upstream = stack_heads(up_buf, g, rows)
            gp = dot_last(upstream, values)
            p_low = probs[block, g]
            p = p_low.astype(F32)
            mean = jnp.sum(p * gp, axis=-1, keepdims=True)
            ds = (p * (gp - mean) * SCALE).astype(BF)
            gq = jnp.dot(ds, keys, preferred_element_type=F32)
            terms = gq * query.astype(F32)
            for h in range(GROUP):
                gn[:, pl.ds((g * GROUP + h) * HD, HD)] = gq[h * rows : (h + 1) * rows]
                inner += terms[h * rows : (h + 1) * rows]
            acc[:, k_cols] = jnp.where(first, 0.0, acc_in[:, k_cols]) + dot_first(
                ds[:, past:], query
            )
            acc[:, v_cols] = jnp.where(first, 0.0, acc_in[:, v_cols]) + dot_first(
                p_low[:, past:], upstream
            )
        grad_rows = acc[mine, :].astype(BF)
        done[mine, :] = grad_rows
        terms = grad_rows.astype(F32) * kv[mine, :].astype(F32)
        for i in range(grad_rows.shape[1] // HD):
            inner += terms[:, i * HD : (i + 1) * HD]
        wide = weight.shape[1]
        inner = jnp.sum(inner, axis=-1, keepdims=True) * (1.0 / wide)
        inv = inv_all[mine, :][:, :1]
        width = WIDTH

        for j in range(wide // width):
            cols = pl.ds(j * width, width)
            part = gn[:, cols] + jnp.dot(grad_rows, weight[:, cols], preferred_element_type=F32)
            grad = (
                up_buf[:, cols].astype(F32)
                + inv * (part - normed_all[mine, cols].astype(F32) * inner)
            ).astype(BF)
            out[:, cols] = grad
            grad_in[mine, cols] = grad


def backward_call(step, rows, sections, info, incoming, cotangent, weight, cached, kept, extra, state):
    fresh = step < SPANS
    wide = weight.shape[1]
    cotangent = cotangent if fresh else incoming
    operands = [incoming, cotangent, weight, cached, *kept, *extra, *state]
    start = 1 + len(operands) - len(state)
    res = pl.pallas_call(
        functools.partial(backward_kernel, step, rows, sections, fresh, len(state), len(extra)),
        out_shape=(pltpu.VMEM((rows, wide), BF), *[vmem_like(a) for a in state]),
        in_specs=[SMEM] + [VMEM] * len(operands),
        out_specs=(VMEM,) * (1 + len(state)),
        scratch_shapes=[pltpu.VMEM((rows, wide), BF), pltpu.VMEM((rows, wide), F32)],
        input_output_aliases={start + i: 1 + i for i in range(len(state))},
        compiler_params=LIMIT,
        name="backward_block",
    )(info, *[in_vmem(a) for a in operands])
    return res[0], res[1:]


YS, XS, CORES = 4, 4, 2
FAR_FIRST, FAR_LAST = (2, 1, 3), (1, 3, 2)


def product_kernel(info, *refs):
    early, columns, grads = refs[: XS - 1], refs[XS - 1 : 2 * XS - 1], refs[2 * XS - 1 : 3 * XS - 1]
    away, mine, left, right = refs[3 * XS - 1 :]
    rows, width = columns[0].shape[0], columns[0].shape[1] // (YS * CORES)
    for d in range(XS):
        part = columns[d][...]
        if d > 0:
            part = jnp.where(info[0] < EARLY, early[d - 1][...], part)
        left[pl.ds(d * rows, rows), :] = part
        right[pl.ds(d * rows, rows), :] = grads[(0, *FAR_LAST).index(d)][...]

    @pl.loop(0, YS)
    def _(j):
        y = lax.rem(info[3] + j, YS)
        for core in range(CORES):
            whose = jnp.where(core == 0, 1 - info[5], info[5])
            cols = pl.ds(pl.multiple_of((y * CORES + whose) * width, width), width)
            part = dot_first(left[:, cols], right[...])
            if core == 0:
                away[j] = part.astype(BF)
            else:
                mine[j] = part


def product_call(info, early, columns, grads):
    rows, pair = grads[0].shape
    width = columns[0].shape[1] // (YS * CORES)
    return pl.pallas_call(
        product_kernel,
        out_shape=(pltpu.VMEM((YS, width, pair), BF), pltpu.VMEM((YS, width, pair), F32)),
        in_specs=[SMEM] + [VMEM] * (3 * XS - 1),
        out_specs=(VMEM, VMEM),
        scratch_shapes=[
            pltpu.VMEM((XS * rows, columns[0].shape[1]), BF),
            pltpu.VMEM((XS * rows, pair), BF),
        ],
        compiler_params=LIMIT,
        name="document_product",
    )(info, *[in_vmem(a) for a in (*early, *columns, *grads)])


def merge_kernel(mine, other, *parts):
    parts[0][...] = mine[0] + other[0].astype(F32)
    for j in range(1, YS):
        parts[j][...] = (mine[j] + other[j].astype(F32)).astype(BF)


def merge_call(mine, other):
    shape = mine.shape[1:]
    return pl.pallas_call(
        merge_kernel,
        out_shape=tuple(pltpu.VMEM(shape, F32 if j == 0 else BF) for j in range(YS)),
        in_specs=[VMEM, VMEM],
        out_specs=(VMEM,) * YS,
        compiler_params=LIMIT,
        name="merge_cores",
    )(in_vmem(mine), in_vmem(other))


def from_offset(value, axis, by):
    size = lax.axis_size(axis)
    return lax.ppermute(value, axis, [((i + by) % size, i) for i in range(size)])


def columns_from(pieces, members):
    found = []
    for d in range(1, XS):
        pairs = [(s * XS + (i + d) % XS, s * XS + i) for s in members for i in range(XS)]
        found.append(lax.ppermute(pieces[XS - d], ("section", "x"), pairs))
    return found


def summed_share(info, early, columns, grad_rows):
    moved = {d: from_offset(grad_rows, "x", d) for d in FAR_LAST}
    grads = [grad_rows] + [moved[d] for d in FAR_LAST]
    away, mine = product_call(info, early, columns, grads)
    total, *parts = merge_call(mine, from_offset(away, "core", 1))
    moved = {j: from_offset(parts[j - 1], "y", -j) for j in FAR_FIRST}
    for j in FAR_FIRST:
        total = total + moved[j].astype(F32)
    return total


def body(tokens, kv_weight, cache_kv, cached_len, cotangent):
    at = lax.axis_index("section")
    sections = lax.axis_size("section")
    total, wide = tokens.shape[1:]
    pair = kv_weight.shape[2]
    rows = total // SPANS
    past = cache_kv.shape[2]
    steps = LAG * (sections - 1) + SPANS
    where = [lax.axis_index(axis) for axis in ("y", "x", "core")]
    info = jnp.stack([at, cached_len[0], sections - 1, *where]).astype(jnp.int32)

    def hop(value, step, by):
        window = range(step - step % WINDOW, step - step % WINDOW + WINDOW)
        movers = [
            (s, s + by)
            for s in range(sections)
            if 0 <= s + by < sections
            and any(0 <= t - LAG * (s if by > 0 else sections - 1 - s) < SPANS for t in window)
        ]
        needed = step < LAG * (sections - 2) + SPANS
        return lax.ppermute(value, "section", movers) if needed else None

    weight, cached, stream, upstream, *spare = load_call(
        info,
        [kv_weight[0], cache_kv[0, 0], tokens[0], cotangent[0]],
        [
            pltpu.VMEM((total, pair), BF),
            pltpu.VMEM((total, HD), F32),
            pltpu.VMEM((total, wide), BF),
            pltpu.VMEM((total, wide), BF),
            pltpu.VMEM((SPANS, KV_HEADS, GROUP * rows, past + total), BF),
            pltpu.VMEM((total, pair), F32),
            pltpu.VMEM((total, wide), BF),
            pltpu.VMEM((total, pair), BF),
            pltpu.VMEM((rows, wide), BF),
        ]
        + [pltpu.VMEM((total, wide // XS), BF)] * XS
        + [pltpu.VMEM((pair, wide), BF)],
    )
    state, back, empty, pieces, turned = spare[:5], spare[5:8], spare[8], spare[9:-1], spare[-1]
    state = [*state, turned]

    arrived = [empty] * LAG
    for step in range(steps):
        if step == steps - SPANS - LAG:
            state = [*state, *pieces]
        block_out, state = forward_call(step, rows, info, arrived[step], stream, weight, cached, state)
        arrived.append(hop(block_out, step, 1))
        state, pieces = state[:6], state[6:] or pieces
    kv, inv, normed, hidden, probs, turned = state
    early = columns_from(pieces, range(EARLY))
    wanted = {2 * i + 3: [piece] for i, piece in enumerate(early)}

    arrived = [empty] * LAG
    for step in range(steps):
        turn = step == LAG * (sections - 1 - EARLY) + SPANS
        if turn:
            back = [*back, *pieces]
        block_grad, back = backward_call(
            step, rows, sections, info, arrived[step], upstream, turned, cached, (kv, inv, normed, probs),
            wanted.get(step, []), back,
        )
        arrived.append(hop(block_grad, step, -1))
        if turn:
            back, pieces = back[:3], back[3:]
            late = columns_from(pieces, range(EARLY, sections))
            wanted = {step + 2 * i + 3: [piece] for i, piece in enumerate(late)}
    _, grad_in, done = back
    columns = [pieces[0], *late]
    share = summed_share(info, early, columns, done)
    return (hidden[None, None], grad_in[None, None], share[None])


def solution(mesh):
    devices = mesh.devices.reshape(-1, YS, XS, CORES)
    dp = ("y", "x", "core")
    return jax.shard_map(
        body,
        mesh=Mesh(devices, ("section",) + dp),
        in_specs=(
            P(dp, None, None),
            P("section", None, None),
            P("section", dp, None, None),
            P(dp),
            P(dp, None, None),
        ),
        out_specs=(
            P("section", dp, None, None),
            P("section", dp, None, None),
            P("section", dp, None),
        ),
        check_vma=False,
    )
```
